128 devices in a mesh: row: 8 (over y_lo, x), rhs: 16 (over y_hi, z, core).
Axes of the slice: x: 4, y: 4 (y_hi: 2, y_lo: 2; y = y_hi * 2 + y_lo), z: 4, core: 2. Of those that a mesh axis runs over, the one named last changes fastest.
Arguments:
- factor: float32 [6144, 24, 256], P('row', None, 'rhs'), as said below
- inverses: float32 [24, 256, 256], P('row'), as said below
- right_side: float32 [6144, 8192], P('row', 'rhs'), may hold values from -6 to 6
Outputs:
- solution: float32 [6144, 8192], P('row', 'rhs')
The draws below stay inside these ranges and needn't reach their ends.
Inputs may be any that keep to these rules, and one draw needn't show every extreme that they name: factor[i, j, c] is zero unless j is less than i // 256. Each inverses[p] is lower triangular with a positive diagonal.
All inputs are finite; a program needn't handle non-finite values.
Results may differ from the reference program's by a relative error of at most 0.0001.
Values sent between devices are 32-bit elements; how exact they have to be, the bound alone decides.
A program may use at most 128 MiB of HBM per device.

```python
import jax
import jax.numpy as jnp
from jax import lax

PANEL = 256
WIN = 6144
NP = 24
NRHS = 8192


def draw_factor(key, part):
    rows = jnp.arange(WIN, dtype=jnp.int32) // PANEL
    cols = jnp.arange(NP, dtype=jnp.int32)
    keep = (cols[None, :] < rows[:, None]).astype(jnp.float32)
    start = jnp.maximum(rows * PANEL, 1).astype(jnp.float32)
    values = jax.random.normal(key, (WIN, NP, PANEL), jnp.float32)
    scales = 0.5
    return values * scales * keep[:, :, None] / jnp.sqrt(start)[:, None, None]


def draw_inverses(key, part):
    lower = jnp.tril(jnp.ones((PANEL, PANEL), jnp.float32), -1)
    values = jax.random.normal(key, (NP, PANEL, PANEL), jnp.float32)
    diag = jax.random.uniform(jax.random.fold_in(key, 3), (NP, PANEL), jnp.float32, 0.6, 1.4)
    return values * lower[None] * (0.5 / jnp.sqrt(PANEL * 1.0)) + diag[:, :, None] * jnp.eye(PANEL, dtype=jnp.float32)[None]


def shard_levels(own_key, extent, cuts, least, top_value):
    loudness = 1.0
    for position, parts in cuts:
        steps = jax.random.uniform(jax.random.fold_in(jax.random.fold_in(own_key, 6), position), (parts,), jnp.float32, least / len(cuts), top_value / len(cuts))
        loudness = loudness * jnp.repeat(jnp.exp(steps), extent[position] // parts).reshape((-1,) + (1,) * (len(extent) - 1 - position))
    return loudness


def bell_draw(key, extent, scale, most, split=(), kind=jnp.bfloat16):
    array = scale * jax.random.normal(key, extent, jnp.float32)
    if split:
        array = array * shard_levels(key, extent, split, -0.22, 0.18)
    return jnp.clip(array, -most, most).astype(kind)


def setup_inputs(seed: int = 0) -> dict:
    key_of = jax.random.split(jax.random.key(seed), 4)
    factor = draw_factor(jax.random.fold_in(key_of[3], 71), 0)
    inverses = draw_inverses(jax.random.fold_in(key_of[3], 71), 0)
    right_side = bell_draw(key_of[2], (WIN, NRHS), 1.0, 6.0, ((0, 8), (1, 16)), jnp.float32)
    return {"factor": factor, "inverses": inverses, "right_side": right_side}


def mult(left, right):
    return jnp.dot(left, right, preferred_element_type=jnp.float32, precision=lax.Precision.HIGHEST)


def reference(factor, inverses, right_side):
    residual = right_side
    pieces = []
    for step in range(NP):
        solved = mult(inverses[step], residual[:PANEL])
        pieces.append(solved)
        residual = residual[PANEL:] - mult(factor[(step + 1) * PANEL:, step, :], solved)
    return jnp.concatenate(pieces, axis=0)
```

```python
import functools

import jax
import jax.numpy as jnp
from jax import lax
from jax.experimental import pallas as pl
from jax.experimental.pallas import tpu as pltpu
from jax.sharding import PartitionSpec as P

MESH = pl.DeviceIdType.MESH
CHUNKS = 4
F32, BF16 = jnp.float32, jnp.bfloat16


def split(v):
    hi = v.astype(BF16)
    return hi, (v - hi.astype(F32)).astype(BF16)


def dot(a, b):
    return jnp.dot(a, b, preferred_element_type=F32)


def mult(v, wh, wl):
    hi, lo = split(v)
    m = v.shape[0]
    both = dot(jnp.concatenate([hi, lo], axis=0), wh)
    return both[:m] + (both[m:] + dot(hi, wl))


def kernel(
    n, factor, inverses, right, out,
    land, lh, ll, xb, res, sums, ih, il,
    own_sem, send_y, send_z, send_f, send_c, recv_l, recv_c,
    send_x, send_xf, recv_x, send_s, recv_s,
):
    row, rhs = lax.axis_index("row"), lax.axis_index("rhs")
    group, x = row // 4, row % 4
    yh, z, core = rhs // 8, (rhs // 2) % 4, rhs % 2
    is_a = group == 0
    is_b = group == 1
    panel = inverses.shape[1]
    block, cols = right.shape
    width = cols // n
    up_z, down_z = (z + 1) % 4, (z + 3) % 4
    right_x, left_x = (x + 1) % 4, (x + 3) % 4
    count = jnp.where(is_a, x + 5, x + 1)

    def place(group_, x_, yh_, z_, core_):
        return (group_ * 4 + x_, (yh_ * 4 + z_) * 2 + core_)

    partner = place(group, x, 1 - yh, z, core)
    above, below = place(group, x, yh, up_z, core), place(group, x, yh, down_z, core)
    twin = place(group, x, yh, z, 1 - core)
    east, west = place(group, right_x, yh, z, core), place(group, left_x, yh, z, core)
    cross = place(1 - group, x, yh, z, core)
    cross_far = place(1 - group, x, 1 - yh, z, core)

    def remote(src, dst, send, recv, device):
        return pltpu.make_async_remote_copy(
            src_ref=src, dst_ref=dst, send_sem=send, recv_sem=recv, device_id=device, device_id_type=MESH
        )

    barrier = pltpu.get_barrier_semaphore()
    for device in (partner, above, below, twin, east, west, cross, cross_far):
        pl.semaphore_signal(barrier, inc=1, device_id=device, device_id_type=MESH)
    pl.semaphore_wait(barrier, 8)

    def shard(slot, yh_, z_):
        return land.at[slot, core, :, yh_ * 4 + z_]

    def panels(index):
        return factor.at[pl.ds(3 * index, 3)]

    def send_shard(src, slot, yh_, z_, send, device):
        return remote(src, shard(slot, yh_, z_), send, recv_l.at[slot, yh_ * 4 + z_], device)

    def got_shard(slot, yh_, z_):
        send_shard(shard(slot, yh_, z_), slot, yh_, z_, send_c.at[0], partner).wait_recv()

    def own_copy(slot):
        return pltpu.make_async_copy(panels(4 * group + slot), shard(slot, yh, z), own_sem.at[slot])

    def open_own(slot, carry):
        src = panels(4 * group + slot)
        send_shard(src, slot, yh, z, send_y.at[slot, 0], partner).start()
        send_shard(src, slot, yh, z, send_z.at[slot, yh, 0], above).start()
        send_shard(src, slot, yh, z, send_z.at[slot, yh, 1], below).start()
        own_copy(slot).start()
        return carry

    def open_cross(s, carry):
        send_shard(panels(s), 4 + s, yh, z, send_y.at[4 + s, 0], cross).start()
        send_shard(panels(s), 4 + s, yh, z, send_y.at[4 + s, 1], cross_far).start()
        return carry

    lax.fori_loop(0, x + 1, open_own, 0)

    @pl.when(is_b)
    def _():
        lax.fori_loop(0, 4, open_cross, 0)

    def slot_of(v):
        return jnp.where(v <= x, v, 3 - x + v)

    def pass_on(slot, yh_):
        got_shard(slot, yh_, z)
        send_shard(shard(slot, yh_, z), slot, yh_, z, send_z.at[slot, yh_, 0], above).start()
        send_shard(shard(slot, yh_, z), slot, yh_, z, send_z.at[slot, yh_, 1], below).start()

    def far_up(slot):
        return send_shard(shard(slot, yh, down_z), slot, yh, down_z, send_f.at[slot, 0], above)

    def far_down(slot):
        return send_shard(shard(slot, 1 - yh, up_z), slot, 1 - yh, up_z, send_f.at[slot, 1], below)

    def to_twin(slot):
        return remote(land.at[slot, core], land.at[slot, core], send_c.at[slot], recv_c.at[slot], twin)

    def halves(slot):
        def piece(i, carry):
            p, yz = i // 8, i % 8
            for c in range(2):
                hi, lo = split(land[slot, c, p, yz])
                rows = hi.shape[0]
                at = pl.ds(pl.multiple_of((i * 2 + c) * rows, rows), rows)
                lh[slot, at, :] = hi
                ll[slot, at, :] = lo
            return carry

        lax.fori_loop(0, 24, piece, 0)

    def serve(v):
        def inside(u):
            return jnp.logical_and(u >= 0, u < count)

        @pl.when(inside(v + 3))
        def _():
            slot = slot_of(v + 3)
            pass_on(slot, 1 - yh)

            @pl.when(v + 3 > x)
            def _():
                pass_on(slot, yh)

        @pl.when(inside(v + 2))
        def _():
            slot = slot_of(v + 2)
            got_shard(slot, yh, down_z)
            far_up(slot).start()
            got_shard(slot, 1 - yh, up_z)
            far_down(slot).start()

        @pl.when(inside(v + 1))
        def _():
            slot = slot_of(v + 1)

            @pl.when(v + 1 <= x)
            def _():
                own_copy(slot).wait()

            got_shard(slot, 1 - yh, down_z)
            got_shard(slot, yh, up_z)
            got_shard(slot, yh, (z + 2) % 4)
            got_shard(slot, 1 - yh, (z + 2) % 4)
            to_twin(slot).start()

        @pl.when(inside(v))
        def _():
            slot = slot_of(v)
            remote(land.at[slot, 1 - core], land.at[slot, 1 - core], send_c.at[slot], recv_c.at[slot], twin).wait_recv()
            halves(slot)

    def send_own_x(c, way):
        device = (east, west)[way]
        return remote(xb.at[x, c], xb.at[x, c], send_x.at[c, way], recv_x.at[x, c], device)

    own_east = jnp.logical_or(is_a, x < 3)
    own_west = jnp.logical_or(is_a, x == 0)
    far_east = jnp.logical_or(is_a, jnp.logical_or(x == 1, x == 2))

    def forward_x(c):
        return remote(xb.at[left_x, c], xb.at[left_x, c], send_xf.at[c], recv_x.at[left_x, c], east)

    def got_x(j, c):
        remote(xb.at[j, c], xb.at[j, c], send_xf.at[c], recv_x.at[j, c], east).wait_recv()

        @pl.when(jnp.logical_and(j == left_x, far_east))
        def _():
            forward_x(c).start()

    def send_sum(c):
        return remote(sums.at[c], sums.at[c], send_s.at[c], recv_s.at[c], cross)

    def update(c, j):
        hi, lo = split(xb[j, c])
        both = jnp.concatenate([hi, lo], axis=0)
        for t in range(3):
            at = slice(t * panel, (t + 1) * panel)
            first = dot(both, lh[j, :, at])
            res[c, :, at] -= first[:width] + (first[width:] + dot(hi, ll[j, :, at]))

    def solve(c):
        @pl.when(is_b)
        def _():
            remote(sums.at[c], sums.at[c], send_s.at[c], recv_s.at[c], cross).wait_recv()
            res[c] = res[c] - sums[c]

        one, two = slice(panel, 2 * panel), slice(2 * panel, 3 * panel)
        x0 = mult(res[c, :, :panel], ih[0], il[0])
        xb[x, c, :, :panel] = x0
        rest = res[c, :, panel:] - mult(x0, lh[x, :panel, panel:], ll[x, :panel, panel:])
        x1 = mult(rest[:, :panel], ih[1], il[1])
        xb[x, c, :, one] = x1
        last = rest[:, panel:] - mult(x1, lh[x, one, two], ll[x, one, two])
        xb[x, c, :, two] = mult(last, ih[2], il[2])

        @pl.when(own_east)
        def _():
            send_own_x(c, 0).start()

        @pl.when(own_west)
        def _():
            send_own_x(c, 1).start()

        out[:, pl.ds(pl.multiple_of(c * width, width), width)] = xb[x, c].T

    for p in range(3):
        hi, lo = split(inverses[p].T)
        ih[p] = hi
        il[p] = lo

    def flip(c, carry):
        res[c] = right[:, pl.ds(pl.multiple_of(c * width, width), width)].T
        return carry

    lax.fori_loop(0, n, flip, 0)

    for v in (-3, -2, -1):
        serve(v)

    def chunk(c, carry):
        @pl.when(jnp.logical_and(c > 0, x + c < count))
        def _():
            serve(x + c)

        def earlier(j, carry):
            @pl.when(c == 0)
            def _():
                serve(j)

            @pl.when(j < x)
            def _():
                got_x(j, c)
                update(c, j)

            return carry

        lax.fori_loop(0, jnp.where(c == 0, x + 1, x), earlier, 0)
        solve(c)
        return carry

    lax.fori_loop(0, n, chunk, 0)

    @pl.when(is_a)
    def _():
        for v in range(n, 5):
            serve(x + v)

        def total(c, carry):
            def term(j, carry):
                @pl.when(j > x)
                def _():
                    got_x(j, c)

                hi, lo = split(xb[j, c])
                both = jnp.concatenate([hi, lo], axis=0)
                for t in range(3):
                    at = slice(t * panel, (t + 1) * panel)
                    first = dot(both, lh[4 + j, :, at])
                    value = first[:width] + (first[width:] + dot(hi, ll[4 + j, :, at]))
                    sums[c, :, at] = jnp.where(j == 0, 0.0, sums[c, :, at]) + value
                return carry

            lax.fori_loop(0, 4, term, 0)
            send_sum(c).start()
            return carry

        lax.fori_loop(0, n, total, 0)

    def sent_slot(v, carry):
        slot = slot_of(v)

        @pl.when(v <= x)
        def _():
            send_shard(shard(slot, yh, z), slot, yh, z, send_y.at[slot, 0], partner).wait_send()

        for a in range(2):
            for way in range(2):
                send_shard(shard(slot, yh, z), slot, yh, z, send_z.at[slot, a, way], above).wait_send()
        far_up(slot).wait_send()
        far_down(slot).wait_send()
        to_twin(slot).wait_send()
        return carry

    lax.fori_loop(0, count, sent_slot, 0)

    @pl.when(is_b)
    def _():
        def sent_cross(s, carry):
            for far in range(2):
                send_shard(panels(s), 4 + s, yh, z, send_y.at[4 + s, far], cross).wait_send()
            return carry

        lax.fori_loop(0, 4, sent_cross, 0)

    def sent_x(c, carry):
        @pl.when(own_east)
        def _():
            send_own_x(c, 0).wait_send()

        @pl.when(own_west)
        def _():
            send_own_x(c, 1).wait_send()

        @pl.when(far_east)
        def _():
            forward_x(c).wait_send()

        @pl.when(is_a)
        def _():
            send_sum(c).wait_send()

        return carry

    lax.fori_loop(0, n, sent_x, 0)


def body(factor, inverses, right_side):
    n = CHUNKS
    block, cols = right_side.shape
    panel = inverses.shape[1]
    part = factor.shape[2]
    width = cols // n
    turned = jnp.transpose(factor, (1, 2, 0))
    dma = pltpu.SemaphoreType.DMA
    vmem = pl.BlockSpec(memory_space=pltpu.VMEM)
    return pl.pallas_call(
        functools.partial(kernel, n),
        out_shape=jax.ShapeDtypeStruct((block, cols), F32),
        in_specs=[pl.BlockSpec(memory_space=pl.ANY), vmem, vmem],
        out_specs=vmem,
        scratch_shapes=[
            pltpu.VMEM((8, 2, 3, 8, part, block), F32),
            pltpu.VMEM((8, block, block), BF16),
            pltpu.VMEM((8, block, block), BF16),
            pltpu.VMEM((4, n, width, block), F32),
            pltpu.VMEM((n, width, block), F32),
            pltpu.VMEM((n, width, block), F32),
            pltpu.VMEM((3, panel, panel), BF16),
            pltpu.VMEM((3, panel, panel), BF16),
            dma((4,)),
            dma((8, 2)),
            dma((8, 2, 2)),
            dma((8, 2)),
            dma((8,)),
            dma((8, 8)),
            dma((8,)),
            dma((n, 2)),
            dma((n,)),
            dma((4, n)),
            dma((n,)),
            dma((n,)),
        ],
        compiler_params=pltpu.CompilerParams(
            collective_id=0, has_side_effects=True, vmem_limit_bytes=60 * 1024 * 1024
        ),
    )(turned, inverses, right_side)


def solution(mesh):
    placed = (P("row", None, "rhs"), P("row", None, None), P("row", "rhs"))
    return jax.shard_map(
        body, mesh=mesh, in_specs=placed, out_specs=P("row", "rhs"), check_vma=False
    )
```

```python
import functools

import jax
import jax.numpy as jnp
from jax import lax
from jax.experimental import pallas as pl
from jax.experimental.pallas import tpu as pltpu
from jax.sharding import PartitionSpec as P

MESH = pl.DeviceIdType.MESH
CHUNKS = 8
KEPT = 2
F32, BF16 = jnp.float32, jnp.bfloat16


def split(v):
    hi = v.astype(BF16)
    return hi, (v - hi.astype(F32)).astype(BF16)


def dot(a, b):
    return jnp.dot(a, b, preferred_element_type=F32)


def mult(v, wh, wl):
    hi, lo = split(v)
    m = v.shape[0]
    both = dot(jnp.concatenate([hi, lo], axis=0), wh)
    return both[:m] + (both[m:] + dot(hi, wl))


def kernel(
    n, factor, inverses, right, out,
    land, lh, ll, xb, res, sums, ih, il,
    own_sem, send_y, send_b, send_z, send_f, send_c, recv_l, recv_c,
    send_x, send_xf, recv_x, send_s, recv_s,
):
    row, rhs = lax.axis_index("row"), lax.axis_index("rhs")
    group, x = row // 4, row % 4
    yh, z, core = rhs // 8, (rhs // 2) % 4, rhs % 2
    is_a = group == 0
    is_b = group == 1
    panel = inverses.shape[1]
    block, cols = right.shape
    width = cols // n
    per = max(1, 128 // width)
    up_z, down_z = (z + 1) % 4, (z + 3) % 4
    right_x, left_x = (x + 1) % 4, (x + 3) % 4
    count = jnp.where(is_a, x + 5, x + 1)

    def place(group_, x_, yh_, z_, core_):
        return (group_ * 4 + x_, (yh_ * 4 + z_) * 2 + core_)

    partner = place(group, x, 1 - yh, z, core)
    above, below = place(group, x, yh, up_z, core), place(group, x, yh, down_z, core)
    twin = place(group, x, yh, z, 1 - core)
    east, west = place(group, right_x, yh, z, core), place(group, left_x, yh, z, core)
    cross = place(1 - group, x, yh, z, core)
    cross_far = place(1 - group, x, 1 - yh, z, core)

    def remote(src, dst, send, recv, device):
        return pltpu.make_async_remote_copy(
            src_ref=src, dst_ref=dst, send_sem=send, recv_sem=recv, device_id=device, device_id_type=MESH
        )

    barrier = pltpu.get_barrier_semaphore()
    for device in (partner, above, below, twin, east, west, cross, cross_far):
        pl.semaphore_signal(barrier, inc=1, device_id=device, device_id_type=MESH)
    pl.semaphore_wait(barrier, 8)

    def shard(slot, yh_, z_):
        return land.at[slot, core, :, yh_ * 4 + z_]

    def panels(index):
        return factor.at[pl.ds(3 * index, 3)]

    def send_shard(src, slot, yh_, z_, send, device):
        return remote(src, shard(slot, yh_, z_), send, recv_l.at[slot, yh_ * 4 + z_], device)

    def got_shard(slot, yh_, z_):
        send_shard(shard(slot, yh_, z_), slot, yh_, z_, send_c.at[0], partner).wait_recv()

    def own_copy(slot):
        return pltpu.make_async_copy(panels(4 * group + slot), shard(slot, yh, z), own_sem.at[slot])

    def open_own(slot, carry):
        src = panels(4 * group + slot)
        send_shard(src, slot, yh, z, send_y.at[slot, 0], partner).start()
        send_shard(src, slot, yh, z, send_z.at[slot, yh, 0], above).start()
        send_shard(src, slot, yh, z, send_z.at[slot, yh, 1], below).start()
        own_copy(slot).start()
        return carry

    def over_y(src, s, z_, far):
        return send_shard(src, 4 + s, yh, z_, send_b.at[s, z_, far], (cross, cross_far)[far])

    def open_cross(s, carry):
        over_y(panels(s), s, z, 0).start()
        over_y(panels(s), s, z, 1).start()

        @pl.when(s >= KEPT)
        def _():
            send_shard(panels(s), 4 + s, yh, z, send_z.at[4 + s, yh, 0], above).start()
            send_shard(panels(s), 4 + s, yh, z, send_z.at[4 + s, yh, 1], below).start()

        return carry

    def far_cross(s, way):
        came, to = ((down_z, above), (up_z, below))[way]
        return send_shard(shard(4 + s, yh, came), 4 + s, yh, came, send_f.at[4 + s, 0], to)

    def cross_near(s, carry):
        for way, came in ((0, down_z), (1, up_z)):
            got_shard(4 + s, yh, came)

            @pl.when(s % 2 == way)
            def _():
                far_cross(s, way).start()

            for far in range(2):
                over_y(shard(4 + s, yh, came), s, came, far).start()
        return carry

    def cross_last(s, carry):
        came = (z + 2) % 4
        got_shard(4 + s, yh, came)
        for far in range(2):
            over_y(shard(4 + s, yh, came), s, came, far).start()
        return carry

    @pl.when(is_b)
    def _():
        lax.fori_loop(0, 4, open_cross, 0)

    lax.fori_loop(0, x + 1, open_own, 0)

    def slot_of(v):
        return jnp.where(v <= x, v, 3 - x + v)

    def pass_on(slot, yh_):
        got_shard(slot, yh_, z)
        send_shard(shard(slot, yh_, z), slot, yh_, z, send_z.at[slot, yh_, 0], above).start()
        send_shard(shard(slot, yh_, z), slot, yh_, z, send_z.at[slot, yh_, 1], below).start()

    def far_up(slot):
        return send_shard(shard(slot, yh, down_z), slot, yh, down_z, send_f.at[slot, 0], above)

    def far_down(slot):
        return send_shard(shard(slot, 1 - yh, up_z), slot, 1 - yh, up_z, send_f.at[slot, 1], below)

    def to_twin(slot):
        return remote(land.at[slot, core], land.at[slot, core], send_c.at[slot], recv_c.at[slot], twin)

    def halves(slot):
        def piece(i, carry):
            p, yz = i // 8, i % 8
            for c in range(2):
                hi, lo = split(land[slot, c, p, yz])
                rows = hi.shape[0]
                at = pl.ds(pl.multiple_of((i * 2 + c) * rows, rows), rows)
                lh[slot, at, :] = hi
                ll[slot, at, :] = lo
            return carry

        lax.fori_loop(0, 24, piece, 0)

    def serve(v):
        def inside(u):
            return jnp.logical_and(u >= 0, u < count)

        def relayed(u):
            return jnp.logical_and(inside(u), u < x + 1 + KEPT)

        @pl.when(relayed(v + 3))
        def _():
            slot = slot_of(v + 3)
            pass_on(slot, 1 - yh)

            @pl.when(v + 3 > x)
            def _():
                pass_on(slot, yh)

        @pl.when(relayed(v + 2))
        def _():
            slot = slot_of(v + 2)
            got_shard(slot, yh, down_z)
            far_up(slot).start()
            got_shard(slot, 1 - yh, up_z)
            far_down(slot).start()

        @pl.when(inside(v + 1))
        def _():
            slot = slot_of(v + 1)

            @pl.when(v + 1 <= x)
            def _():
                own_copy(slot).wait()

            @pl.when(v + 1 > x + KEPT)
            def _():
                got_shard(slot, yh, z)
                got_shard(slot, 1 - yh, z)
                got_shard(slot, yh, down_z)
                got_shard(slot, 1 - yh, up_z)

            got_shard(slot, 1 - yh, down_z)
            got_shard(slot, yh, up_z)
            got_shard(slot, yh, (z + 2) % 4)
            got_shard(slot, 1 - yh, (z + 2) % 4)
            to_twin(slot).start()

        @pl.when(inside(v))
        def _():
            slot = slot_of(v)
            remote(land.at[slot, 1 - core], land.at[slot, 1 - core], send_c.at[slot], recv_c.at[slot], twin).wait_recv()
            halves(slot)

    def send_own_x(c, way):
        device = (east, west)[way]
        return remote(xb.at[x, c], xb.at[x, c], send_x.at[c, way], recv_x.at[x, c], device)

    own_east = jnp.logical_or(is_a, x < 3)

    def own_west(c):
        return jnp.logical_or(is_a, jnp.logical_or(x == 0, jnp.logical_and(x == 1, c % 2 == 1)))

    def far_east(c):
        low = jnp.logical_and(jnp.logical_or(x == 1, x == 2), c % 2 == 0)
        return jnp.logical_or(low, jnp.logical_and(is_a, jnp.logical_or(x == 0, x == 3)))

    def far_west(c):
        return jnp.logical_and(jnp.logical_or(x == 0, x == 3), c % 2 == 1)

    def forward_x(j, c, way):
        return remote(xb.at[j, c], xb.at[j, c], send_xf.at[c, way], recv_x.at[j, c], (east, west)[way])

    def got_x(j, c):
        remote(xb.at[j, c], xb.at[j, c], send_x.at[c, 0], recv_x.at[j, c], east).wait_recv()

        @pl.when(jnp.logical_and(j == left_x, far_east(c)))
        def _():
            forward_x(j, c, 0).start()

        @pl.when(jnp.logical_and(j == right_x, far_west(c)))
        def _():
            forward_x(j, c, 1).start()

    def early_x(i):
        @pl.when(jnp.logical_and(x == 3, i + 1 < n))
        def _():
            @pl.when(i == 0)
            def _():
                got_x(0, 0)

            got_x(0, i + 1)

        mine = jnp.logical_and(x == 0, jnp.logical_or(is_a, i % 2 == 1))

        @pl.when(jnp.logical_and(mine, i >= 2))
        def _():
            got_x(1, i - 2)

    def early(j):
        return jnp.logical_or(jnp.logical_and(x == 3, j == 0), jnp.logical_and(x == 0, j == 1))

    def send_sum(c):
        return remote(sums.at[c], sums.at[c], send_s.at[c], recv_s.at[c], cross)

    def update(c, j):
        hi, lo = split(xb[j, c])
        both = jnp.concatenate([hi, lo], axis=0)
        for t in range(3):
            at = slice(t * panel, (t + 1) * panel)
            first = dot(both, lh[j, :, at])
            res[c, :, at] -= first[:width] + (first[width:] + dot(hi, ll[j, :, at]))

    def solve(c):
        @pl.when(is_b)
        def _():
            remote(sums.at[c], sums.at[c], send_s.at[c], recv_s.at[c], cross).wait_recv()
            res[c] = res[c] - sums[c]

        one, two = slice(panel, 2 * panel), slice(2 * panel, 3 * panel)
        x0 = mult(res[c, :, :panel], ih[0], il[0])
        xb[x, c, :, :panel] = x0
        rest = res[c, :, panel:] - mult(x0, lh[x, :panel, panel:], ll[x, :panel, panel:])
        x1 = mult(rest[:, :panel], ih[1], il[1])
        xb[x, c, :, one] = x1
        last = rest[:, panel:] - mult(x1, lh[x, one, two], ll[x, one, two])
        xb[x, c, :, two] = mult(last, ih[2], il[2])

        @pl.when(own_east)
        def _():
            send_own_x(c, 0).start()

        @pl.when(own_west(c))
        def _():
            send_own_x(c, 1).start()

        @pl.when(c % per == per - 1)
        def _():
            both = xb[x, pl.ds(c - (per - 1), per)].reshape(per * width, block)
            out[:, pl.ds(pl.multiple_of((c // per) * per * width, per * width), per * width)] = both.T

    for p in range(3):
        hi, lo = split(inverses[p].T)
        ih[p] = hi
        il[p] = lo

    def flip(i, carry):
        turned = right[:, pl.ds(pl.multiple_of(i * per * width, per * width), per * width)].T
        res[pl.ds(i * per, per)] = turned.reshape(per, width, block)
        return carry

    lax.fori_loop(0, n // per, flip, 0)

    @pl.when(is_b)
    def _():
        lax.fori_loop(KEPT, 4, cross_near, 0)
        lax.fori_loop(KEPT, 4, cross_last, 0)

    for v in (-3, -2, -1):
        serve(v)

    def chunk(c, carry):
        early_x(c)

        def earlier(j, carry):
            @pl.when(c == 0)
            def _():
                serve(j)

            @pl.when(j < x)
            def _():
                @pl.when(jnp.logical_not(early(j)))
                def _():
                    got_x(j, c)

                update(c, j)

            return carry

        lax.fori_loop(0, jnp.where(c == 0, x + 1, x), earlier, 0)
        solve(c)
        return carry

    lax.fori_loop(0, n, chunk, 0)
    for i in (n, n + 1):
        early_x(i)

    @pl.when(is_a)
    def _():
        def term(j, carry):
            serve(x + 1 + j)

            def total(c, carry):
                @pl.when(jnp.logical_and(j > x, jnp.logical_not(early(j))))
                def _():
                    got_x(j, c)

                hi, lo = split(xb[j, c])
                both = jnp.concatenate([hi, lo], axis=0)
                for t in range(3):
                    at = slice(t * panel, (t + 1) * panel)
                    first = dot(both, lh[4 + j, :, at])
                    value = first[:width] + (first[width:] + dot(hi, ll[4 + j, :, at]))
                    sums[c, :, at] = jnp.where(j == 0, 0.0, sums[c, :, at]) + value

                @pl.when(j == 3)
                def _():
                    send_sum(c).start()

                return carry

            lax.fori_loop(0, n, total, 0)
            return carry

        lax.fori_loop(0, 4, term, 0)

    def sent_slot(v, carry):
        slot = slot_of(v)

        @pl.when(v <= x)
        def _():
            send_shard(shard(slot, yh, z), slot, yh, z, send_y.at[slot, 0], partner).wait_send()

        @pl.when(v < x + 1 + KEPT)
        def _():
            for a in range(2):
                for way in range(2):
                    send_shard(shard(slot, yh, z), slot, yh, z, send_z.at[slot, a, way], above).wait_send()
            far_up(slot).wait_send()
            far_down(slot).wait_send()

        to_twin(slot).wait_send()
        return carry

    lax.fori_loop(0, count, sent_slot, 0)

    @pl.when(is_b)
    def _():
        def sent_cross(s, carry):
            for far in range(2):
                over_y(panels(s), s, z, far).wait_send()

            @pl.when(s >= KEPT)
            def _():
                for way in range(2):
                    send_shard(panels(s), 4 + s, yh, z, send_z.at[4 + s, yh, way], above).wait_send()
                far_cross(s, 0).wait_send()
                for come in (up_z, down_z, (z + 2) % 4):
                    for far in range(2):
                        over_y(panels(s), s, come, far).wait_send()

            return carry

        lax.fori_loop(0, 4, sent_cross, 0)

    def sent_x(c, carry):
        @pl.when(own_east)
        def _():
            send_own_x(c, 0).wait_send()

        @pl.when(own_west(c))
        def _():
            send_own_x(c, 1).wait_send()

        @pl.when(far_east(c))
        def _():
            forward_x(x, c, 0).wait_send()

        @pl.when(far_west(c))
        def _():
            forward_x(x, c, 1).wait_send()

        @pl.when(is_a)
        def _():
            send_sum(c).wait_send()

        return carry

    lax.fori_loop(0, n, sent_x, 0)


def body(factor, inverses, right_side):
    n = CHUNKS
    block, cols = right_side.shape
    panel = inverses.shape[1]
    part = factor.shape[2]
    width = cols // n
    turned = jnp.transpose(factor, (1, 2, 0))
    dma = pltpu.SemaphoreType.DMA
    vmem = pl.BlockSpec(memory_space=pltpu.VMEM)
    return pl.pallas_call(
        functools.partial(kernel, n),
        out_shape=jax.ShapeDtypeStruct((block, cols), F32),
        in_specs=[pl.BlockSpec(memory_space=pl.ANY), vmem, vmem],
        out_specs=vmem,
        scratch_shapes=[
            pltpu.VMEM((8, 2, 3, 8, part, block), F32),
            pltpu.VMEM((8, block, block), BF16),
            pltpu.VMEM((8, block, block), BF16),
            pltpu.VMEM((4, n, width, block), F32),
            pltpu.VMEM((n, width, block), F32),
            pltpu.VMEM((n, width, block), F32),
            pltpu.VMEM((3, panel, panel), BF16),
            pltpu.VMEM((3, panel, panel), BF16),
            dma((4,)),
            dma((4, 1)),
            dma((4, 4, 2)),
            dma((8, 2, 2)),
            dma((8, 2)),
            dma((8,)),
            dma((8, 8)),
            dma((8,)),
            dma((n, 2)),
            dma((n, 2)),
            dma((4, n)),
            dma((n,)),
            dma((n,)),
        ],
        compiler_params=pltpu.CompilerParams(
            collective_id=0, has_side_effects=True, vmem_limit_bytes=60 * 1024 * 1024
        ),
    )(turned, inverses, right_side)


def solution(mesh):
    placed = (P("row", None, "rhs"), P("row", None, None), P("row", "rhs"))
    return jax.shard_map(
        body, mesh=mesh, in_specs=placed, out_specs=P("row", "rhs"), check_vma=False
    )
```

```python
import functools

import jax
import jax.numpy as jnp
from jax import lax
from jax.experimental import pallas as pl
from jax.experimental.pallas import tpu as pltpu
from jax.sharding import PartitionSpec as P

MESH = pl.DeviceIdType.MESH
CHUNKS = 8
F32, BF16 = jnp.float32, jnp.bfloat16


def split(v):
    hi = v.astype(BF16)
    return hi, (v - hi.astype(F32)).astype(BF16)


def dot(a, b):
    return jnp.dot(a, b, preferred_element_type=F32)


def mult(v, wh, wl):
    hi, lo = split(v)
    m = v.shape[0]
    both = dot(jnp.concatenate([hi, lo], axis=0), wh)
    return both[:m] + (both[m:] + dot(hi, wl))


def kernel(
    n, factor, inverses, right, out,
    land, lh, ll, xb, res, sums, ih, il,
    own_sem, send_y, send_b, send_z, send_f, send_c, recv_l, recv_c,
    send_x, send_xf, recv_x, send_s, recv_s,
):
    row, rhs = lax.axis_index("row"), lax.axis_index("rhs")
    group, x = row // 4, row % 4
    yh, z, core = rhs // 8, (rhs // 2) % 4, rhs % 2
    is_a = group == 0
    is_b = group == 1
    panel = inverses.shape[1]
    block, cols = right.shape
    width = cols // n
    per = max(1, 128 // width)
    up_z, down_z = (z + 1) % 4, (z + 3) % 4
    right_x, left_x = (x + 1) % 4, (x + 3) % 4
    kept = jnp.where(x == 0, 3, jnp.where(x == 3, 1, 2))

    def place(group_, x_, yh_, z_, core_):
        return (group_ * 4 + x_, (yh_ * 4 + z_) * 2 + core_)

    partner = place(group, x, 1 - yh, z, core)
    above, below = place(group, x, yh, up_z, core), place(group, x, yh, down_z, core)
    twin = place(group, x, yh, z, 1 - core)
    east, west = place(group, right_x, yh, z, core), place(group, left_x, yh, z, core)
    cross = place(1 - group, x, yh, z, core)
    cross_far = place(1 - group, x, 1 - yh, z, core)

    def remote(src, dst, send, recv, device):
        return pltpu.make_async_remote_copy(
            src_ref=src, dst_ref=dst, send_sem=send, recv_sem=recv, device_id=device, device_id_type=MESH
        )

    barrier = pltpu.get_barrier_semaphore()
    for device in (partner, above, below, twin, east, west, cross, cross_far):
        pl.semaphore_signal(barrier, inc=1, device_id=device, device_id_type=MESH)
    pl.semaphore_wait(barrier, 8)

    def shard(slot, yh_, z_):
        return land.at[slot, core, :, yh_ * 4 + z_]

    def panels(index):
        return factor.at[pl.ds(3 * index, 3)]

    def send_shard(src, slot, yh_, z_, send, device):
        return remote(src, shard(slot, yh_, z_), send, recv_l.at[slot, yh_ * 4 + z_], device)

    def got_shard(slot, yh_, z_):
        send_shard(shard(slot, yh_, z_), slot, yh_, z_, send_c.at[0], partner).wait_recv()

    def own_copy(slot):
        return pltpu.make_async_copy(panels(4 * group + slot), shard(slot, yh, z), own_sem.at[slot])

    def open_own(slot, carry):
        src = panels(4 * group + slot)
        send_shard(src, slot, yh, z, send_y.at[slot, 0], partner).start()
        send_shard(src, slot, yh, z, send_z.at[slot, yh, 0], above).start()
        send_shard(src, slot, yh, z, send_z.at[slot, yh, 1], below).start()
        own_copy(slot).start()
        return carry

    def over_y(src, s, z_, far):
        return send_shard(src, 4 + s, yh, z_, send_b.at[s, z_, far], (cross, cross_far)[far])

    def open_cross(s, carry):
        over_y(panels(s), s, z, 0).start()
        over_y(panels(s), s, z, 1).start()

        @pl.when(s >= kept)
        def _():
            send_shard(panels(s), 4 + s, yh, z, send_z.at[4 + s, yh, 0], above).start()
            send_shard(panels(s), 4 + s, yh, z, send_z.at[4 + s, yh, 1], below).start()

        return carry

    def far_cross(s, way):
        came, to = ((down_z, above), (up_z, below))[way]
        return send_shard(shard(4 + s, yh, came), 4 + s, yh, came, send_f.at[4 + s, 0], to)

    def cross_near(s, carry):
        for way, came in ((0, down_z), (1, up_z)):
            got_shard(4 + s, yh, came)

            @pl.when(s % 2 == way)
            def _():
                far_cross(s, way).start()

            for far in range(2):
                over_y(shard(4 + s, yh, came), s, came, far).start()
        return carry

    def cross_last(s, carry):
        came = (z + 2) % 4
        got_shard(4 + s, yh, came)
        for far in range(2):
            over_y(shard(4 + s, yh, came), s, came, far).start()
        return carry

    @pl.when(is_b)
    def _():
        lax.fori_loop(0, 4, open_cross, 0)

    lax.fori_loop(0, x + 1, open_own, 0)

    def pass_on(slot, yh_):
        got_shard(slot, yh_, z)
        send_shard(shard(slot, yh_, z), slot, yh_, z, send_z.at[slot, yh_, 0], above).start()
        send_shard(shard(slot, yh_, z), slot, yh_, z, send_z.at[slot, yh_, 1], below).start()

    def far_up(slot):
        return send_shard(shard(slot, yh, down_z), slot, yh, down_z, send_f.at[slot, 0], above)

    def far_down(slot):
        return send_shard(shard(slot, 1 - yh, up_z), slot, 1 - yh, up_z, send_f.at[slot, 1], below)

    def to_twin(slot):
        return remote(land.at[slot, core], land.at[slot, core], send_c.at[slot], recv_c.at[slot], twin)

    def halves(slot):
        def piece(i, carry):
            p, yz = i // 8, i % 8
            for c in range(2):
                hi, lo = split(land[slot, c, p, yz])
                rows = hi.shape[0]
                at = pl.ds(pl.multiple_of((i * 2 + c) * rows, rows), rows)
                lh[slot, at, :] = hi
                ll[slot, at, :] = lo
            return carry

        lax.fori_loop(0, 24, piece, 0)

    def far_on(slot):
        got_shard(slot, yh, down_z)
        far_up(slot).start()
        got_shard(slot, 1 - yh, up_z)
        far_down(slot).start()

    def far_here(slot):
        got_shard(slot, 1 - yh, down_z)
        got_shard(slot, yh, up_z)
        got_shard(slot, yh, (z + 2) % 4)
        got_shard(slot, 1 - yh, (z + 2) % 4)

    def finish(slot):
        remote(land.at[slot, 1 - core], land.at[slot, 1 - core], send_c.at[slot], recv_c.at[slot], twin).wait_recv()
        halves(slot)

    def pass_on_cross(s, carry):
        pass_on(4 + s, 0)
        pass_on(4 + s, 1)
        return carry

    def close_cross(s, carry):
        @pl.when(s >= kept)
        def _():
            got_shard(4 + s, yh, z)
            got_shard(4 + s, 1 - yh, z)
            got_shard(4 + s, yh, down_z)
            got_shard(4 + s, 1 - yh, up_z)

        far_here(4 + s)
        to_twin(4 + s).start()

        @pl.when(s > 0)
        def _():
            finish(3 + s)

        return carry

    def send_own_x(c, way):
        device = (east, west)[way]
        return remote(xb.at[x, c], xb.at[x, c], send_x.at[c, way], recv_x.at[x, c], device)

    own_east = jnp.logical_or(is_a, x < 3)

    def own_west(c):
        return jnp.logical_or(is_a, jnp.logical_or(x == 0, jnp.logical_and(x == 1, c % 2 == 1)))

    def far_east(c):
        on_a = jnp.logical_or(x == 0, jnp.logical_and(x == 2, c < 2))
        on_b = jnp.logical_and(x == 2, c % 2 == 0)
        return jnp.logical_or(jnp.logical_and(is_a, on_a), jnp.logical_and(is_b, on_b))

    def far_west(c):
        on_a = jnp.logical_or(x == 1, jnp.logical_and(x == 0, c >= 2))
        on_b = jnp.logical_and(x == 0, c % 2 == 1)
        either = jnp.logical_or(jnp.logical_and(is_a, on_a), jnp.logical_and(is_b, on_b))
        return jnp.logical_or(x == 3, either)

    def forward_x(j, c, way):
        return remote(xb.at[j, c], xb.at[j, c], send_xf.at[c, way], recv_x.at[j, c], (east, west)[way])

    def got_x(j, c):
        remote(xb.at[j, c], xb.at[j, c], send_x.at[c, 0], recv_x.at[j, c], east).wait_recv()

        @pl.when(jnp.logical_and(j == left_x, far_east(c)))
        def _():
            forward_x(j, c, 0).start()

        @pl.when(jnp.logical_and(j == right_x, far_west(c)))
        def _():
            forward_x(j, c, 1).start()

    step = n // 4

    def early_group(v):
        @pl.when(jnp.logical_and(is_a, x == 3))
        def _():
            for k in range(step):
                got_x(0, v * step + k)

        @pl.when(jnp.logical_and(jnp.logical_and(is_a, x == 2), v >= 1))
        def _():
            got_x(1, v - 1)

    def early_x(i):
        @pl.when(jnp.logical_and(jnp.logical_and(is_b, x == 3), i + 1 < n))
        def _():
            @pl.when(i == 0)
            def _():
                got_x(0, 0)

            got_x(0, i + 1)

        @pl.when(jnp.logical_and(jnp.logical_and(is_b, x == 0), jnp.logical_and(i >= 3, i % 2 == 0)))
        def _():
            got_x(1, i - 3)

        @pl.when(jnp.logical_and(jnp.logical_and(is_a, x == 1), i >= n - 2))
        def _():
            got_x(2, i - (n - 2))

    def early(j, c):
        second = jnp.logical_and(jnp.logical_and(is_a, x == 2), jnp.logical_and(j == 1, c < 2))
        return jnp.logical_or(jnp.logical_and(x == 3, j == 0), second)

    def send_sum(c):
        return remote(sums.at[c], sums.at[c], send_s.at[c], recv_s.at[c], cross)

    def update(c, j):
        hi, lo = split(xb[j, c])
        both = jnp.concatenate([hi, lo], axis=0)
        for t in range(3):
            at = slice(t * panel, (t + 1) * panel)
            first = dot(both, lh[j, :, at])
            res[c, :, at] -= first[:width] + (first[width:] + dot(hi, ll[j, :, at]))

    def solve(c):
        @pl.when(is_b)
        def _():
            remote(sums.at[c], sums.at[c], send_s.at[c], recv_s.at[c], cross).wait_recv()
            res[c] = res[c] - sums[c]

        one, two = slice(panel, 2 * panel), slice(2 * panel, 3 * panel)
        x0 = mult(res[c, :, :panel], ih[0], il[0])
        xb[x, c, :, :panel] = x0
        rest = res[c, :, panel:] - mult(x0, lh[x, :panel, panel:], ll[x, :panel, panel:])
        x1 = mult(rest[:, :panel], ih[1], il[1])
        xb[x, c, :, one] = x1
        last = rest[:, panel:] - mult(x1, lh[x, one, two], ll[x, one, two])
        xb[x, c, :, two] = mult(last, ih[2], il[2])

        @pl.when(own_east)
        def _():
            send_own_x(c, 0).start()

        @pl.when(own_west(c))
        def _():
            send_own_x(c, 1).start()

        @pl.when(c % per == per - 1)
        def _():
            both = xb[x, pl.ds(c - (per - 1), per)].reshape(per * width, block)
            out[:, pl.ds(pl.multiple_of((c // per) * per * width, per * width), per * width)] = both.T

    for p in range(3):
        hi, lo = split(inverses[p].T)
        ih[p] = hi
        il[p] = lo

    def flip(i, carry):
        turned = right[:, pl.ds(pl.multiple_of(i * per * width, per * width), per * width)].T
        res[pl.ds(i * per, per)] = turned.reshape(per, width, block)
        return carry

    lax.fori_loop(0, n // per, flip, 0)

    @pl.when(is_b)
    def _():
        lax.fori_loop(kept, 4, cross_near, 0)
        lax.fori_loop(kept, 4, cross_last, 0)

    def own_group(v, carry):
        @pl.when(v + 2 <= x)
        def _():
            pass_on(v + 2, 1 - yh)

        @pl.when(v + 1 <= x)
        def _():
            far_on(v + 1)

        return carry

    pass_on(0, 1 - yh)

    @pl.when(x >= 1)
    def _():
        pass_on(1, 1 - yh)

    far_on(0)

    def one_chunk(c, first):
        early_x(c)

        def earlier(j, carry):
            if first:
                own_copy(j).wait()
                far_here(j)
                to_twin(j).start()
                finish(j)
                early_group(j)

            @pl.when(j < x)
            def _():
                @pl.when(jnp.logical_not(early(j, c)))
                def _():
                    got_x(j, c)

                update(c, j)

            if first:
                own_group(j, 0)

                @pl.when(jnp.logical_and(is_a, j == x - 1))
                def _():
                    lax.fori_loop(0, kept, pass_on_cross, 0)

            return carry

        lax.fori_loop(0, x + 1 if first else x, earlier, 0)
        solve(c)

        @pl.when(jnp.logical_and(jnp.logical_and(is_a, x > 0), jnp.logical_and(c % 2 == 1, c // 2 < kept)))
        def _():
            far_on(4 + c // 2)

    def chunk(c, carry):
        one_chunk(c, False)
        return carry

    one_chunk(0, True)
    lax.fori_loop(1, n, chunk, 0)
    for i in range(n, n + 3):

        @pl.when(is_b)
        def _():
            early_x(i)

    @pl.when(is_a)
    def _():
        @pl.when(x == 0)
        def _():
            def far_cross_group(s, carry):
                far_on(4 + s)
                return carry

            lax.fori_loop(0, kept, pass_on_cross, 0)
            lax.fori_loop(0, kept, far_cross_group, 0)

        lax.fori_loop(0, 4, close_cross, 0)
        finish(7)
        ahead = jnp.where(x == 1, 2, 0)
        behind = jnp.where(x == 0, n // 2, 0)

        def total(i, carry):
            @pl.when(jnp.logical_and(x < 2, i + ahead < n))
            def _():
                got_x(x + 1, i + ahead)

            c = i - behind

            @pl.when(jnp.logical_and(c >= 0, c < n))
            def _():
                def term(j, carry):
                    @pl.when(jnp.logical_and(j > x, jnp.logical_or(x >= 2, j > x + 1)))
                    def _():
                        got_x(j, c)

                    hi, lo = split(xb[j, c])
                    both = jnp.concatenate([hi, lo], axis=0)
                    for t in range(3):
                        at = slice(t * panel, (t + 1) * panel)
                        first = dot(both, lh[4 + j, :, at])
                        value = first[:width] + (first[width:] + dot(hi, ll[4 + j, :, at]))
                        sums[c, :, at] = jnp.where(j == 0, 0.0, sums[c, :, at]) + value
                    return carry

                lax.fori_loop(0, 4, term, 0)
                send_sum(c).start()

            return carry

        lax.fori_loop(0, n + behind, total, 0)

    def sent_ring(slot):
        for a in range(2):
            for way in range(2):
                send_shard(shard(slot, yh, z), slot, yh, z, send_z.at[slot, a, way], above).wait_send()
        far_up(slot).wait_send()
        far_down(slot).wait_send()

    def sent_own(slot, carry):
        send_shard(shard(slot, yh, z), slot, yh, z, send_y.at[slot, 0], partner).wait_send()
        sent_ring(slot)
        to_twin(slot).wait_send()
        return carry

    lax.fori_loop(0, x + 1, sent_own, 0)

    @pl.when(is_a)
    def _():
        def sent_used(s, carry):
            @pl.when(s < kept)
            def _():
                sent_ring(4 + s)

            to_twin(4 + s).wait_send()
            return carry

        lax.fori_loop(0, 4, sent_used, 0)

    @pl.when(is_b)
    def _():
        def sent_cross(s, carry):
            for far in range(2):
                over_y(panels(s), s, z, far).wait_send()

            @pl.when(s >= kept)
            def _():
                for way in range(2):
                    send_shard(panels(s), 4 + s, yh, z, send_z.at[4 + s, yh, way], above).wait_send()
                far_cross(s, 0).wait_send()
                for come in (up_z, down_z, (z + 2) % 4):
                    for far in range(2):
                        over_y(panels(s), s, come, far).wait_send()

            return carry

        lax.fori_loop(0, 4, sent_cross, 0)

    def sent_x(c, carry):
        @pl.when(own_east)
        def _():
            send_own_x(c, 0).wait_send()

        @pl.when(own_west(c))
        def _():
            send_own_x(c, 1).wait_send()

        @pl.when(far_east(c))
        def _():
            forward_x(x, c, 0).wait_send()

        @pl.when(far_west(c))
        def _():
            forward_x(x, c, 1).wait_send()

        @pl.when(is_a)
        def _():
            send_sum(c).wait_send()

        return carry

    lax.fori_loop(0, n, sent_x, 0)


def body(factor, inverses, right_side):
    n = CHUNKS
    block, cols = right_side.shape
    panel = inverses.shape[1]
    part = factor.shape[2]
    width = cols // n
    turned = jnp.transpose(factor, (1, 2, 0))
    dma = pltpu.SemaphoreType.DMA
    vmem = pl.BlockSpec(memory_space=pltpu.VMEM)
    return pl.pallas_call(
        functools.partial(kernel, n),
        out_shape=jax.ShapeDtypeStruct((block, cols), F32),
        in_specs=[pl.BlockSpec(memory_space=pl.ANY), vmem, vmem],
        out_specs=vmem,
        scratch_shapes=[
            pltpu.VMEM((8, 2, 3, 8, part, block), F32),
            pltpu.VMEM((8, block, block), BF16),
            pltpu.VMEM((8, block, block), BF16),
            pltpu.VMEM((4, n, width, block), F32),
            pltpu.VMEM((n, width, block), F32),
            pltpu.VMEM((n, width, block), F32),
            pltpu.VMEM((3, panel, panel), BF16),
            pltpu.VMEM((3, panel, panel), BF16),
            dma((4,)),
            dma((4, 1)),
            dma((4, 4, 2)),
            dma((8, 2, 2)),
            dma((8, 2)),
            dma((8,)),
            dma((8, 8)),
            dma((8,)),
            dma((n, 2)),
            dma((n, 2)),
            dma((4, n)),
            dma((n,)),
            dma((n,)),
        ],
        compiler_params=pltpu.CompilerParams(
            collective_id=0, has_side_effects=True, vmem_limit_bytes=60 * 1024 * 1024
        ),
    )(turned, inverses, right_side)


def solution(mesh):
    placed = (P("row", None, "rhs"), P("row", None, None), P("row", "rhs"))
    return jax.shard_map(
        body, mesh=mesh, in_specs=placed, out_specs=P("row", "rhs"), check_vma=False
    )
```

```python
import functools

import jax
import jax.numpy as jnp
from jax import lax
from jax.experimental import pallas as pl
from jax.experimental.pallas import tpu as pltpu
from jax.sharding import PartitionSpec as P

MESH = pl.DeviceIdType.MESH
CHUNKS = 8
LEAD = 3
BEHIND2 = 4
BEHIND3 = 2
F32, BF16 = jnp.float32, jnp.bfloat16


def split(v):
    hi = v.astype(BF16)
    return hi, (v - hi.astype(F32)).astype(BF16)


def dot(a, b):
    return jnp.dot(a, b, preferred_element_type=F32)


def mult(v, wh, wl):
    hi, lo = split(v)
    m = v.shape[0]
    both = dot(jnp.concatenate([hi, lo], axis=0), wh)
    return both[:m] + (both[m:] + dot(hi, wl))


def kernel(
    n, factor, inverses, right, out,
    land, lh, ll, xb, res, sums, ih, il,
    own_sem, send_y, send_b, send_z, send_f, send_c, recv_l, recv_c,
    send_x, send_xf, recv_x, send_s, recv_s,
):
    row, rhs = lax.axis_index("row"), lax.axis_index("rhs")
    group, x = row // 4, row % 4
    yh, z, core = rhs // 8, (rhs // 2) % 4, rhs % 2
    is_a = group == 0
    is_b = group == 1
    panel = inverses.shape[1]
    block, cols = right.shape
    width = cols // n
    per = max(1, 128 // width)
    up_z, down_z = (z + 1) % 4, (z + 3) % 4
    right_x, left_x = (x + 1) % 4, (x + 3) % 4
    kept = jnp.where(x == 0, 3, jnp.where(x == 3, 1, 2))

    def place(group_, x_, yh_, z_, core_):
        return (group_ * 4 + x_, (yh_ * 4 + z_) * 2 + core_)

    partner = place(group, x, 1 - yh, z, core)
    above, below = place(group, x, yh, up_z, core), place(group, x, yh, down_z, core)
    twin = place(group, x, yh, z, 1 - core)
    east, west = place(group, right_x, yh, z, core), place(group, left_x, yh, z, core)
    cross = place(1 - group, x, yh, z, core)
    cross_far = place(1 - group, x, 1 - yh, z, core)

    def remote(src, dst, send, recv, device):
        return pltpu.make_async_remote_copy(
            src_ref=src, dst_ref=dst, send_sem=send, recv_sem=recv, device_id=device, device_id_type=MESH
        )

    def shard(slot, yh_, z_, k=3):
        return land.at[slot, core, pl.ds(0, k), yh_ * 4 + z_]

    def panels(index):
        return factor.at[pl.ds(3 * index, 3)]

    def send_shard(src, slot, yh_, z_, send, device, k=3):
        return remote(src, shard(slot, yh_, z_, k), send, recv_l.at[slot, yh_ * 4 + z_], device)

    def got_shard(slot, yh_, z_, k=3):
        send_shard(shard(slot, yh_, z_, k), slot, yh_, z_, send_c.at[0], partner, k).wait_recv()

    def relay(slot, yh_, z_, send, device, k=3):
        return send_shard(shard(slot, yh_, z_, k), slot, yh_, z_, send, device, k)

    def own_copy(slot):
        return pltpu.make_async_copy(panels(4 * group + slot), shard(slot, yh, z), own_sem.at[slot])

    def corner(k):
        first = 3 * (4 * group + x)
        here = land.at[x, core, 0, yh * 4 + z]
        if k == 0:
            src, dst = factor.at[first, :, pl.ds(panel, 2 * panel)], here.at[:, pl.ds(panel, 2 * panel)]
        else:
            src, dst = factor.at[first + 1, :, pl.ds(2 * panel, panel)], here.at[:, pl.ds(0, panel)]
        return pltpu.make_async_copy(src, dst, own_sem.at[4 + k])

    def open_own(slot, carry):
        src = panels(4 * group + slot)
        send_shard(src, slot, yh, z, send_y.at[slot, z], partner).start()
        send_shard(src, slot, yh, z, send_z.at[slot, yh, 0], above).start()
        send_shard(src, slot, yh, z, send_z.at[slot, yh, 1], below).start()
        own_copy(slot).start()
        return carry

    def open_corner():
        corner(0).wait()
        corner(1).wait()
        relay(x, yh, z, send_y.at[x, z], partner, 1).start()
        relay(x, yh, z, send_z.at[x, yh, 0], above, 1).start()
        relay(x, yh, z, send_z.at[x, yh, 1], below, 1).start()

    def along_first(slot):
        return jnp.logical_and(jnp.logical_and(slot >= 1, slot <= 2), slot < x)

    def ring_one(slot, way):
        came, to = ((down_z, above), (up_z, below))[way]
        return relay(slot, yh, came, send_f.at[slot, 0], to)

    def along_near(slot):
        for way, came in ((0, down_z), (1, up_z)):
            got_shard(slot, yh, came)

            @pl.when(slot % 2 == way)
            def _():
                ring_one(slot, way).start()

            relay(slot, yh, came, send_y.at[slot, came], partner).start()

    def along_last(slot):
        came = (z + 2) % 4
        got_shard(slot, yh, came)
        relay(slot, yh, came, send_y.at[slot, came], partner).start()

    corner(0).start()
    corner(1).start()
    barrier = pltpu.get_barrier_semaphore()
    for device in (partner, above, below, twin, east, west, cross, cross_far):
        pl.semaphore_signal(barrier, inc=1, device_id=device, device_id_type=MESH)
    pl.semaphore_wait(barrier, 8)

    def over_y(src, s, z_, far):
        return send_shard(src, 4 + s, yh, z_, send_b.at[s, z_, far], (cross, cross_far)[far])

    def open_cross(s, carry):
        over_y(panels(s), s, z, 0).start()
        over_y(panels(s), s, z, 1).start()

        @pl.when(s >= kept)
        def _():
            send_shard(panels(s), 4 + s, yh, z, send_z.at[4 + s, yh, 0], above).start()
            send_shard(panels(s), 4 + s, yh, z, send_z.at[4 + s, yh, 1], below).start()

        return carry

    def far_cross(s, way):
        came, to = ((down_z, above), (up_z, below))[way]
        return send_shard(shard(4 + s, yh, came), 4 + s, yh, came, send_f.at[4 + s, 0], to)

    def cross_near(s, carry):
        for way, came in ((0, down_z), (1, up_z)):
            got_shard(4 + s, yh, came)

            @pl.when(s % 2 == way)
            def _():
                far_cross(s, way).start()

            for far in range(2):
                over_y(shard(4 + s, yh, came), s, came, far).start()
        return carry

    def cross_last(s, carry):
        came = (z + 2) % 4
        got_shard(4 + s, yh, came)
        for far in range(2):
            over_y(shard(4 + s, yh, came), s, came, far).start()
        return carry

    @pl.when(is_b)
    def _():
        lax.fori_loop(0, 4, open_cross, 0)

    lax.fori_loop(0, x, open_own, 0)
    open_corner()

    def pass_on(slot, yh_, k=3):
        got_shard(slot, yh_, z, k)
        relay(slot, yh_, z, send_z.at[slot, yh_, 0], above, k).start()
        relay(slot, yh_, z, send_z.at[slot, yh_, 1], below, k).start()

    def far_up(slot, k=3):
        return relay(slot, yh, down_z, send_f.at[slot, 0], above, k)

    def far_down(slot, k=3):
        return relay(slot, 1 - yh, up_z, send_f.at[slot, 1], below, k)

    def to_twin(slot, k=3):
        part = land.at[slot, core, pl.ds(0, k)]
        return remote(part, part, send_c.at[slot], recv_c.at[slot], twin)

    def halves(slot, k=3):
        def piece(i, carry):
            p, yz = i // 8, i % 8
            for c in range(2):
                hi, lo = split(land[slot, c, p, yz])
                rows = hi.shape[0]
                at = pl.ds(pl.multiple_of((i * 2 + c) * rows, rows), rows)
                lh[slot, at, :] = hi
                ll[slot, at, :] = lo
            return carry

        lax.fori_loop(0, 8 * k, piece, 0)

    def far_on(slot, k=3):
        got_shard(slot, yh, down_z, k)
        far_up(slot, k).start()
        got_shard(slot, 1 - yh, up_z, k)
        far_down(slot, k).start()

    def far_here(slot, k=3):
        got_shard(slot, 1 - yh, down_z, k)
        got_shard(slot, yh, up_z, k)
        got_shard(slot, yh, (z + 2) % 4, k)
        got_shard(slot, 1 - yh, (z + 2) % 4, k)

    def finish(slot, k=3):
        part = land.at[slot, 1 - core, pl.ds(0, k)]
        remote(part, part, send_c.at[slot], recv_c.at[slot], twin).wait_recv()
        halves(slot, k)

    def pass_on_cross(s, carry):
        pass_on(4 + s, 0)
        pass_on(4 + s, 1)
        return carry

    def close_cross(s, carry):
        @pl.when(x == 0)
        def _():
            for k in range(n // 8):
                got_x(1, n // 2 + s * (n // 8) + k)

        @pl.when(s >= kept)
        def _():
            got_shard(4 + s, yh, z)
            got_shard(4 + s, 1 - yh, z)
            got_shard(4 + s, yh, down_z)
            got_shard(4 + s, 1 - yh, up_z)

        far_here(4 + s)
        to_twin(4 + s).start()

        @pl.when(s > 0)
        def _():
            finish(3 + s)

        return carry

    def send_own_x(c, way):
        device = (east, west)[way]
        return remote(xb.at[x, c], xb.at[x, c], send_x.at[c, way], recv_x.at[x, c], device)

    own_east = jnp.logical_or(is_a, x < 3)

    def own_west(c):
        return jnp.logical_or(is_a, jnp.logical_or(x == 0, jnp.logical_and(x == 1, c % 2 == 1)))

    def far_east(c):
        on_a = jnp.logical_or(x == 0, jnp.logical_and(x == 2, c < 2))
        on_b = jnp.logical_and(x == 2, c % 2 == 0)
        return jnp.logical_or(jnp.logical_and(is_a, on_a), jnp.logical_and(is_b, on_b))

    def far_west(c):
        on_a = jnp.logical_or(x == 1, jnp.logical_and(x == 0, c >= 2))
        on_b = jnp.logical_and(x == 0, c % 2 == 1)
        either = jnp.logical_or(jnp.logical_and(is_a, on_a), jnp.logical_and(is_b, on_b))
        return jnp.logical_or(x == 3, either)

    def forward_x(j, c, way):
        return remote(xb.at[j, c], xb.at[j, c], send_xf.at[c, way], recv_x.at[j, c], (east, west)[way])

    def got_x(j, c):
        remote(xb.at[j, c], xb.at[j, c], send_x.at[c, 0], recv_x.at[j, c], east).wait_recv()

        @pl.when(jnp.logical_and(j == left_x, far_east(c)))
        def _():
            forward_x(j, c, 0).start()

        @pl.when(jnp.logical_and(j == right_x, far_west(c)))
        def _():
            forward_x(j, c, 1).start()

    step = n // 4

    def early_group(v):
        @pl.when(jnp.logical_and(is_a, x == 3))
        def _():
            for k in range(step):
                got_x(0, v * step + k)

    def early_x(i):
        @pl.when(jnp.logical_and(jnp.logical_and(is_b, x == 3), i + LEAD < n))
        def _():
            @pl.when(i == 0)
            def _():
                for k in range(LEAD):
                    got_x(0, k)

            got_x(0, i + LEAD)

        @pl.when(jnp.logical_and(jnp.logical_and(is_b, x == 0), jnp.logical_and(i >= 3, i % 2 == 0)))
        def _():
            got_x(1, i - 3)

        @pl.when(jnp.logical_and(jnp.logical_and(is_a, x == 1), i >= n - 2))
        def _():
            got_x(2, i - (n - 2))

    def early(j):
        return jnp.logical_and(x == 3, j == 0)

    def send_sum(c):
        return remote(sums.at[c], sums.at[c], send_s.at[c], recv_s.at[c], cross)

    def update(c, j):
        hi, lo = split(xb[j, c])
        both = jnp.concatenate([hi, lo], axis=0)
        for t in range(3):
            at = slice(t * panel, (t + 1) * panel)
            first = dot(both, lh[j, :, at])
            res[c, :, at] -= first[:width] + (first[width:] + dot(hi, ll[j, :, at]))

    def solve(c):
        @pl.when(is_b)
        def _():
            remote(sums.at[c], sums.at[c], send_s.at[c], recv_s.at[c], cross).wait_recv()
            res[c] = res[c] - sums[c]

        one, two = slice(panel, 2 * panel), slice(2 * panel, 3 * panel)
        x0 = mult(res[c, :, :panel], ih[0], il[0])
        xb[x, c, :, :panel] = x0
        rest = res[c, :, panel:] - mult(x0, lh[x, :panel, panel:], ll[x, :panel, panel:])
        x1 = mult(rest[:, :panel], ih[1], il[1])
        xb[x, c, :, one] = x1
        last = rest[:, panel:] - mult(x1, lh[x, :panel, :panel], ll[x, :panel, :panel])
        xb[x, c, :, two] = mult(last, ih[2], il[2])

        @pl.when(own_east)
        def _():
            send_own_x(c, 0).start()

        @pl.when(own_west(c))
        def _():
            send_own_x(c, 1).start()

        @pl.when(c % per == per - 1)
        def _():
            both = xb[x, pl.ds(c - (per - 1), per)].reshape(per * width, block)
            out[:, pl.ds(pl.multiple_of((c // per) * per * width, per * width), per * width)] = both.T

    for p in range(3):
        hi, lo = split(inverses[p].T)
        ih[p] = hi
        il[p] = lo

    def flip(i, carry):
        turned = right[:, pl.ds(pl.multiple_of(i * per * width, per * width), per * width)].T
        res[pl.ds(i * per, per)] = turned.reshape(per, width, block)
        return carry

    lax.fori_loop(0, n // per, flip, 0)

    @pl.when(is_b)
    def _():
        lax.fori_loop(kept, 4, cross_near, 0)
        lax.fori_loop(kept, 4, cross_last, 0)

    def by_kind(slot, on_corner, on_along, on_plain):
        @pl.when(slot == x)
        def _():
            on_corner()

        @pl.when(slot < x)
        def _():
            along = along_first(slot)

            @pl.when(along)
            def _():
                on_along()

            @pl.when(jnp.logical_not(along))
            def _():
                on_plain()

    def own_near(u):
        by_kind(u, lambda: pass_on(u, 1 - yh, 1), lambda: along_near(u), lambda: pass_on(u, 1 - yh))

    def own_far(u):
        by_kind(u, lambda: far_on(u, 1), lambda: along_last(u), lambda: far_on(u))

    def own_all(u):
        def corner_all():
            far_here(u, 1)
            to_twin(u, 1).start()

        def along_all():
            own_copy(u).wait()
            for z_ in range(4):
                got_shard(u, 1 - yh, z_)
            to_twin(u).start()

        def plain_all():
            own_copy(u).wait()
            far_here(u)
            to_twin(u).start()

        by_kind(u, corner_all, along_all, plain_all)

    def own_group(v, carry):
        own_all(v)
        own_near(v + 2)
        own_far(v + 1)

        @pl.when(jnp.logical_and(is_a, v == x - 1))
        def _():
            lax.fori_loop(0, kept, pass_on_cross, 0)

        by_kind(v, lambda: finish(v, 1), lambda: finish(v), lambda: finish(v))
        early_group(v)
        return carry

    own_near(0)
    own_near(1)
    own_far(0)
    lax.fori_loop(0, x + 1, own_group, 0)

    ahead = jnp.where(x == 1, 2, 0)
    behind = jnp.where(x == 3, BEHIND3, jnp.where(x == 2, BEHIND2, n))

    def total(c, carry):
        @pl.when(jnp.logical_and(x == 1, c + ahead < n))
        def _():
            got_x(x + 1, c + ahead)

        def term(j, carry):
            @pl.when(jnp.logical_and(j > x, jnp.logical_or(x >= 2, j > x + 1)))
            def _():
                got_x(j, c)

            hi, lo = split(xb[j, c])
            both = jnp.concatenate([hi, lo], axis=0)
            for t in range(3):
                at = slice(t * panel, (t + 1) * panel)
                first = dot(both, lh[4 + j, :, at])
                value = first[:width] + (first[width:] + dot(hi, ll[4 + j, :, at]))
                sums[c, :, at] = jnp.where(j == 0, 0.0, sums[c, :, at]) + value
            return carry

        lax.fori_loop(0, 4, term, 0)
        send_sum(c).start()

        return carry

    def close_all():
        lax.fori_loop(0, 4, close_cross, 0)
        finish(7)

    def chunk(c, carry):
        early_x(c)

        def earlier(j, carry):
            @pl.when(j < x)
            def _():
                @pl.when(jnp.logical_not(early(j)))
                def _():
                    got_x(j, c)

                update(c, j)

            return carry

        lax.fori_loop(0, x, earlier, 0)
        solve(c)

        @pl.when(jnp.logical_and(jnp.logical_and(is_a, x > 0), jnp.logical_and(c % 2 == 1, c // 2 < kept)))
        def _():
            far_on(4 + c // 2)

        @pl.when(jnp.logical_and(is_a, c >= behind))
        def _():
            @pl.when(c == behind)
            def _():
                close_all()

            total(c - behind, 0)

        return carry

    lax.fori_loop(0, n, chunk, 0)
    for i in range(n, n + 3):

        @pl.when(is_b)
        def _():
            early_x(i)

    @pl.when(is_a)
    def _():
        @pl.when(x == 0)
        def _():
            def pass_second(c, carry):
                got_x(1, c)
                return carry

            def far_cross_group(s, carry):
                far_on(4 + s)
                return carry

            lax.fori_loop(0, kept, pass_on_cross, 0)
            lax.fori_loop(0, kept - 1, far_cross_group, 0)
            lax.fori_loop(0, n // 2, pass_second, 0)
            lax.fori_loop(kept - 1, kept, far_cross_group, 0)

        @pl.when(x < 2)
        def _():
            close_all()

        lax.fori_loop(n - behind, n, total, 0)

    def sent_ring(slot, k=3):
        for a in range(2):
            for way in range(2):
                relay(slot, yh, z, send_z.at[slot, a, way], above, k).wait_send()
        far_up(slot, k).wait_send()
        far_down(slot, k).wait_send()

    def sent_own(slot, carry):
        def corner_sent():
            relay(slot, yh, z, send_y.at[slot, z], partner, 1).wait_send()
            sent_ring(slot, 1)
            to_twin(slot, 1).wait_send()

        def along_sent():
            for z_ in range(4):
                relay(slot, yh, z, send_y.at[slot, z_], partner).wait_send()
            for way in range(2):
                relay(slot, yh, z, send_z.at[slot, yh, way], above).wait_send()
            ring_one(slot, 0).wait_send()
            to_twin(slot).wait_send()

        def plain_sent():
            relay(slot, yh, z, send_y.at[slot, z], partner).wait_send()
            sent_ring(slot)
            to_twin(slot).wait_send()

        by_kind(slot, corner_sent, along_sent, plain_sent)
        return carry

    lax.fori_loop(0, x + 1, sent_own, 0)

    @pl.when(is_a)
    def _():
        def sent_used(s, carry):
            @pl.when(s < kept)
            def _():
                sent_ring(4 + s)

            to_twin(4 + s).wait_send()
            return carry

        lax.fori_loop(0, 4, sent_used, 0)

    @pl.when(is_b)
    def _():
        def sent_cross(s, carry):
            for far in range(2):
                over_y(panels(s), s, z, far).wait_send()

            @pl.when(s >= kept)
            def _():
                for way in range(2):
                    send_shard(panels(s), 4 + s, yh, z, send_z.at[4 + s, yh, way], above).wait_send()
                far_cross(s, 0).wait_send()
                for come in (up_z, down_z, (z + 2) % 4):
                    for far in range(2):
                        over_y(panels(s), s, come, far).wait_send()

            return carry

        lax.fori_loop(0, 4, sent_cross, 0)

    def sent_x(c, carry):
        @pl.when(own_east)
        def _():
            send_own_x(c, 0).wait_send()

        @pl.when(own_west(c))
        def _():
            send_own_x(c, 1).wait_send()

        @pl.when(far_east(c))
        def _():
            forward_x(x, c, 0).wait_send()

        @pl.when(far_west(c))
        def _():
            forward_x(x, c, 1).wait_send()

        @pl.when(is_a)
        def _():
            send_sum(c).wait_send()

        return carry

    lax.fori_loop(0, n, sent_x, 0)


def body(factor, inverses, right_side):
    n = CHUNKS
    block, cols = right_side.shape
    panel = inverses.shape[1]
    part = factor.shape[2]
    width = cols // n
    turned = jnp.transpose(factor, (1, 2, 0))
    dma = pltpu.SemaphoreType.DMA
    vmem = pl.BlockSpec(memory_space=pltpu.VMEM)
    return pl.pallas_call(
        functools.partial(kernel, n),
        out_shape=jax.ShapeDtypeStruct((block, cols), F32),
        in_specs=[pl.BlockSpec(memory_space=pl.ANY), vmem, vmem],
        out_specs=vmem,
        scratch_shapes=[
            pltpu.VMEM((8, 2, 3, 8, part, block), F32),
            pltpu.VMEM((8, block, block), BF16),
            pltpu.VMEM((8, block, block), BF16),
            pltpu.VMEM((4, n, width, block), F32),
            pltpu.VMEM((n, width, block), F32),
            pltpu.VMEM((n, width, block), F32),
            pltpu.VMEM((3, panel, panel), BF16),
            pltpu.VMEM((3, panel, panel), BF16),
            dma((6,)),
            dma((4, 4)),
            dma((4, 4, 2)),
            dma((8, 2, 2)),
            dma((8, 2)),
            dma((8,)),
            dma((8, 8)),
            dma((8,)),
            dma((n, 2)),
            dma((n, 2)),
            dma((4, n)),
            dma((n,)),
            dma((n,)),
        ],
        compiler_params=pltpu.CompilerParams(
            collective_id=0, has_side_effects=True, vmem_limit_bytes=60 * 1024 * 1024
        ),
    )(turned, inverses, right_side)


def solution(mesh):
    placed = (P("row", None, "rhs"), P("row", None, None), P("row", "rhs"))
    return jax.shard_map(
        body, mesh=mesh, in_specs=placed, out_specs=P("row", "rhs"), check_vma=False
    )
```

```python
import functools

import jax
import jax.numpy as jnp
from jax import lax
from jax.experimental import pallas as pl
from jax.experimental.pallas import tpu as pltpu
from jax.sharding import PartitionSpec as P

MESH = pl.DeviceIdType.MESH
CHUNKS = 16
LEAD = 5
KEPT3 = 1
TAKE = (1, 2, 1, 0)
BEHIND2 = 8
BEHIND3 = 8
F32, BF16 = jnp.float32, jnp.bfloat16


def split(v):
    hi = v.astype(BF16)
    return hi, (v - hi.astype(F32)).astype(BF16)


def dot(a, b):
    return jnp.dot(a, b, preferred_element_type=F32)


def mult(v, wh, wl):
    hi, lo = split(v)
    m = v.shape[0]
    both = dot(jnp.concatenate([hi, lo], axis=0), wh)
    return both[:m] + (both[m:] + dot(hi, wl))


def kernel(
    n, factor, inverses, right, out,
    land, lh, ll, xb, res, sums, ih, il,
    own_sem, send_y, send_b, send_z, send_f, send_c, recv_l, recv_c,
    send_x, send_xf, recv_x, send_s, recv_s,
):
    row, rhs = lax.axis_index("row"), lax.axis_index("rhs")
    group, x = row // 4, row % 4
    yh, z, core = rhs // 8, (rhs // 2) % 4, rhs % 2
    is_a = group == 0
    is_b = group == 1
    panel = inverses.shape[1]
    block, cols = right.shape
    width = cols // n
    per = max(1, 128 // width)
    up_z, down_z = (z + 1) % 4, (z + 3) % 4
    right_x, left_x = (x + 1) % 4, (x + 3) % 4
    kept = jnp.where(x == 3, KEPT3, 2)

    def place(group_, x_, yh_, z_, core_):
        return (group_ * 4 + x_, (yh_ * 4 + z_) * 2 + core_)

    partner = place(group, x, 1 - yh, z, core)
    above, below = place(group, x, yh, up_z, core), place(group, x, yh, down_z, core)
    twin = place(group, x, yh, z, 1 - core)
    east, west = place(group, right_x, yh, z, core), place(group, left_x, yh, z, core)
    cross = place(1 - group, x, yh, z, core)
    cross_far = place(1 - group, x, 1 - yh, z, core)

    def remote(src, dst, send, recv, device):
        return pltpu.make_async_remote_copy(
            src_ref=src, dst_ref=dst, send_sem=send, recv_sem=recv, device_id=device, device_id_type=MESH
        )

    def shard(slot, yh_, z_, k=3):
        return land.at[slot, core, pl.ds(0, k), yh_ * 4 + z_]

    def panels(index):
        return factor.at[pl.ds(3 * index, 3)]

    def send_shard(src, slot, yh_, z_, send, device, k=3):
        return remote(src, shard(slot, yh_, z_, k), send, recv_l.at[slot, yh_ * 4 + z_], device)

    def got_shard(slot, yh_, z_, k=3):
        send_shard(shard(slot, yh_, z_, k), slot, yh_, z_, send_c.at[0], partner, k).wait_recv()

    def relay(slot, yh_, z_, send, device, k=3):
        return send_shard(shard(slot, yh_, z_, k), slot, yh_, z_, send, device, k)

    def own_copy(slot):
        return pltpu.make_async_copy(panels(4 * group + slot), shard(slot, yh, z), own_sem.at[slot])

    def corner(k):
        first = 3 * (4 * group + x)
        here = land.at[x, core, 0, yh * 4 + z]
        if k == 0:
            src, dst = factor.at[first, :, pl.ds(panel, 2 * panel)], here.at[:, pl.ds(panel, 2 * panel)]
        else:
            src, dst = factor.at[first + 1, :, pl.ds(2 * panel, panel)], here.at[:, pl.ds(0, panel)]
        return pltpu.make_async_copy(src, dst, own_sem.at[4 + k])

    def open_own(slot, carry):
        src = panels(4 * group + slot)
        send_shard(src, slot, yh, z, send_y.at[slot, z], partner).start()
        send_shard(src, slot, yh, z, send_z.at[slot, yh, 0], above).start()
        send_shard(src, slot, yh, z, send_z.at[slot, yh, 1], below).start()
        own_copy(slot).start()
        return carry

    def open_corner():
        corner(0).wait()
        corner(1).wait()
        relay(x, yh, z, send_y.at[x, z], partner, 1).start()
        relay(x, yh, z, send_z.at[x, yh, 0], above, 1).start()
        relay(x, yh, z, send_z.at[x, yh, 1], below, 1).start()

    def along_first(slot):
        return jnp.logical_and(jnp.logical_and(slot >= 1, slot <= 2), slot < x)

    def ring_one(slot, way):
        came, to = ((down_z, above), (up_z, below))[way]
        return relay(slot, yh, came, send_f.at[slot, 0], to)

    def along_near(slot):
        for way, came in ((0, down_z), (1, up_z)):
            got_shard(slot, yh, came)

            @pl.when(slot % 2 == way)
            def _():
                ring_one(slot, way).start()

            relay(slot, yh, came, send_y.at[slot, came], partner).start()

    def along_last(slot):
        came = (z + 2) % 4
        got_shard(slot, yh, came)
        relay(slot, yh, came, send_y.at[slot, came], partner).start()

    corner(0).start()
    corner(1).start()
    barrier = pltpu.get_barrier_semaphore()
    for device in (partner, above, below, twin, east, west, cross, cross_far):
        pl.semaphore_signal(barrier, inc=1, device_id=device, device_id_type=MESH)
    pl.semaphore_wait(barrier, 8)

    def over_y(src, s, z_, far):
        return send_shard(src, 4 + s, yh, z_, send_b.at[s, z_, far], (cross, cross_far)[far])

    def open_cross(s, carry):
        over_y(panels(s), s, z, 0).start()
        over_y(panels(s), s, z, 1).start()

        @pl.when(s >= kept)
        def _():
            send_shard(panels(s), 4 + s, yh, z, send_z.at[4 + s, yh, 0], above).start()
            send_shard(panels(s), 4 + s, yh, z, send_z.at[4 + s, yh, 1], below).start()

        return carry

    def far_cross(s, way):
        came, to = ((down_z, above), (up_z, below))[way]
        return send_shard(shard(4 + s, yh, came), 4 + s, yh, came, send_f.at[4 + s, 0], to)

    def cross_near(s, carry):
        for way, came in ((0, down_z), (1, up_z)):
            got_shard(4 + s, yh, came)

            @pl.when(s % 2 == way)
            def _():
                far_cross(s, way).start()

            for far in range(2):
                over_y(shard(4 + s, yh, came), s, came, far).start()
        return carry

    def cross_last(s, carry):
        came = (z + 2) % 4
        got_shard(4 + s, yh, came)
        for far in range(2):
            over_y(shard(4 + s, yh, came), s, came, far).start()
        return carry

    @pl.when(is_b)
    def _():
        lax.fori_loop(0, 4, open_cross, 0)

    lax.fori_loop(0, x, open_own, 0)
    open_corner()

    def pass_on(slot, yh_, k=3):
        got_shard(slot, yh_, z, k)
        relay(slot, yh_, z, send_z.at[slot, yh_, 0], above, k).start()
        relay(slot, yh_, z, send_z.at[slot, yh_, 1], below, k).start()

    def far_up(slot, k=3):
        return relay(slot, yh, down_z, send_f.at[slot, 0], above, k)

    def far_down(slot, k=3):
        return relay(slot, 1 - yh, up_z, send_f.at[slot, 1], below, k)

    def to_twin(slot, k=3):
        part = land.at[slot, core, pl.ds(0, k)]
        return remote(part, part, send_c.at[slot], recv_c.at[slot], twin)

    def halves(slot, k=3):
        def piece(i, carry):
            p, yz = i // 8, i % 8
            for c in range(2):
                hi, lo = split(land[slot, c, p, yz])
                rows = hi.shape[0]
                at = pl.ds(pl.multiple_of((i * 2 + c) * rows, rows), rows)
                lh[slot, at, :] = hi
                ll[slot, at, :] = lo
            return carry

        lax.fori_loop(0, 8 * k, piece, 0)

    def far_on(slot, k=3):
        got_shard(slot, yh, down_z, k)
        far_up(slot, k).start()
        got_shard(slot, 1 - yh, up_z, k)
        far_down(slot, k).start()

    def far_here(slot, k=3):
        got_shard(slot, 1 - yh, down_z, k)
        got_shard(slot, yh, up_z, k)
        got_shard(slot, yh, (z + 2) % 4, k)
        got_shard(slot, 1 - yh, (z + 2) % 4, k)

    def finish(slot, k=3):
        part = land.at[slot, 1 - core, pl.ds(0, k)]
        remote(part, part, send_c.at[slot], recv_c.at[slot], twin).wait_recv()
        halves(slot, k)

    def pass_on_cross(s, carry):
        pass_on(4 + s, 0)
        pass_on(4 + s, 1)
        return carry

    def close_cross(s, carry):
        @pl.when(x == 0)
        def _():
            for k in range(n // 8):
                got_x(1, n // 2 + s * (n // 8) + k)

        @pl.when(s >= kept)
        def _():
            got_shard(4 + s, yh, z)
            got_shard(4 + s, 1 - yh, z)
            got_shard(4 + s, yh, down_z)
            got_shard(4 + s, 1 - yh, up_z)

        far_here(4 + s)
        to_twin(4 + s).start()

        @pl.when(s > 0)
        def _():
            finish(3 + s)

        return carry

    def send_own_x(c, way):
        device = (east, west)[way]
        return remote(xb.at[x, c], xb.at[x, c], send_x.at[c, way], recv_x.at[x, c], device)

    own_east = jnp.logical_or(is_a, x < 3)

    def own_west(c):
        return jnp.logical_or(is_a, jnp.logical_or(x == 0, jnp.logical_and(x == 1, c % 2 == 1)))

    def far_east(c):
        on_a = jnp.logical_or(x == 0, jnp.logical_and(x == 2, c < 2))
        on_b = jnp.logical_and(x == 2, c % 2 == 0)
        return jnp.logical_or(jnp.logical_and(is_a, on_a), jnp.logical_and(is_b, on_b))

    def far_west(c):
        on_a = jnp.logical_or(x == 1, jnp.logical_and(x == 0, c >= 2))
        on_b = jnp.logical_and(x == 0, c % 2 == 1)
        either = jnp.logical_or(jnp.logical_and(is_a, on_a), jnp.logical_and(is_b, on_b))
        return jnp.logical_or(x == 3, either)

    def forward_x(j, c, way):
        return remote(xb.at[j, c], xb.at[j, c], send_xf.at[c, way], recv_x.at[j, c], (east, west)[way])

    def got_x(j, c):
        remote(xb.at[j, c], xb.at[j, c], send_x.at[c, 0], recv_x.at[j, c], east).wait_recv()

        @pl.when(jnp.logical_and(j == left_x, far_east(c)))
        def _():
            forward_x(j, c, 0).start()

        @pl.when(jnp.logical_and(j == right_x, far_west(c)))
        def _():
            forward_x(j, c, 1).start()

    unit = max(1, n // 8)
    taken = sum(TAKE) * unit

    def early_group(v):
        @pl.when(jnp.logical_and(is_a, x == 3))
        def _():
            for at, take in enumerate(TAKE):
                first = sum(TAKE[:at]) * unit

                @pl.when(v == at)
                def _(first=first, take=take):
                    for k in range(take * unit):
                        got_x(0, first + k)

    def early_x(i):
        @pl.when(jnp.logical_and(jnp.logical_and(is_b, x == 3), i + LEAD < n))
        def _():
            @pl.when(i == 0)
            def _():
                for k in range(LEAD):
                    got_x(0, k)

            got_x(0, i + LEAD)

        @pl.when(jnp.logical_and(jnp.logical_and(is_a, x == 3), i + taken < n))
        def _():
            got_x(0, i + taken)

        @pl.when(jnp.logical_and(jnp.logical_and(is_b, x == 0), jnp.logical_and(i >= 3, i % 2 == 0)))
        def _():
            got_x(1, i - 3)

        @pl.when(jnp.logical_and(jnp.logical_and(is_a, x == 1), i >= n - 2))
        def _():
            got_x(2, i - (n - 2))

    def early(j):
        return jnp.logical_and(x == 3, j == 0)

    def send_sum(c):
        return remote(sums.at[c], sums.at[c], send_s.at[c], recv_s.at[c], cross)

    def update(c, j, m):
        hi, lo = split(xb[j, pl.ds(c, m)].reshape(m * width, block))
        both = jnp.concatenate([hi, lo], axis=0)
        for t in range(3):
            at = slice(t * panel, (t + 1) * panel)
            first = dot(both, lh[j, :, at])
            value = first[: m * width] + (first[m * width :] + dot(hi, ll[j, :, at]))
            res[pl.ds(c, m), :, at] -= value.reshape(m, width, panel)

    def solve(c):
        @pl.when(is_b)
        def _():
            @pl.when(c % 2 == 0)
            def _():
                send_sum(c // 2).wait_recv()

            res[c] = res[c] - sums[c // 2, pl.ds(pl.multiple_of(c % 2 * width, width), width)]

        one, two = slice(panel, 2 * panel), slice(2 * panel, 3 * panel)
        x0 = mult(res[c, :, :panel], ih[0], il[0])
        xb[x, c, :, :panel] = x0
        rest = res[c, :, panel:] - mult(x0, lh[x, :panel, panel:], ll[x, :panel, panel:])
        x1 = mult(rest[:, :panel], ih[1], il[1])
        xb[x, c, :, one] = x1
        last = rest[:, panel:] - mult(x1, lh[x, :panel, :panel], ll[x, :panel, :panel])
        xb[x, c, :, two] = mult(last, ih[2], il[2])

        @pl.when(own_east)
        def _():
            send_own_x(c, 0).start()

        @pl.when(own_west(c))
        def _():
            send_own_x(c, 1).start()

        @pl.when(c % per == per - 1)
        def _():
            both = xb[x, pl.ds(c - (per - 1), per)].reshape(per * width, block)
            out[:, pl.ds(pl.multiple_of((c // per) * per * width, per * width), per * width)] = both.T

    for p in range(3):
        hi, lo = split(inverses[p].T)
        ih[p] = hi
        il[p] = lo

    def flip(i, carry):
        turned = right[:, pl.ds(pl.multiple_of(i * per * width, per * width), per * width)].T
        res[pl.ds(i * per, per)] = turned.reshape(per, width, block)
        return carry

    lax.fori_loop(0, n // per, flip, 0)

    @pl.when(is_b)
    def _():
        lax.fori_loop(kept, 4, cross_near, 0)
        lax.fori_loop(kept, 4, cross_last, 0)

    def by_kind(slot, on_corner, on_along, on_plain):
        @pl.when(slot == x)
        def _():
            on_corner()

        @pl.when(slot < x)
        def _():
            along = along_first(slot)

            @pl.when(along)
            def _():
                on_along()

            @pl.when(jnp.logical_not(along))
            def _():
                on_plain()

    def own_near(u):
        by_kind(u, lambda: pass_on(u, 1 - yh, 1), lambda: along_near(u), lambda: pass_on(u, 1 - yh))

    def own_far(u):
        by_kind(u, lambda: far_on(u, 1), lambda: along_last(u), lambda: far_on(u))

    def own_all(u):
        def corner_all():
            far_here(u, 1)
            to_twin(u, 1).start()

        def along_all():
            own_copy(u).wait()
            for z_ in range(4):
                got_shard(u, 1 - yh, z_)
            to_twin(u).start()

        def plain_all():
            own_copy(u).wait()
            far_here(u)
            to_twin(u).start()

        by_kind(u, corner_all, along_all, plain_all)

    def own_group(v, carry):
        own_all(v)

        @pl.when(v > 0)
        def _():
            finish(v - 1)

        early_group(v)
        return carry

    def near_group(u, carry):
        own_near(u)
        return carry

    def far_group(u, carry):
        own_far(u)
        return carry

    lax.fori_loop(0, x + 1, near_group, 0)
    lax.fori_loop(0, x + 1, far_group, 0)

    @pl.when(jnp.logical_and(is_a, x > 0))
    def _():
        lax.fori_loop(0, kept, pass_on_cross, 0)

    lax.fori_loop(0, x + 1, own_group, 0)
    finish(x, 1)

    ahead = jnp.where(x == 1, 2, 0)
    behind = jnp.where(x == 3, BEHIND3, jnp.where(x == 2, BEHIND2, n))

    def total(m, carry):
        for k in range(2):

            @pl.when(jnp.logical_and(x == 1, 2 * m + k + ahead < n))
            def _(k=k):
                got_x(x + 1, 2 * m + k + ahead)

        def term(j, carry):
            @pl.when(jnp.logical_and(j > x, jnp.logical_or(x >= 2, j > x + 1)))
            def _():
                got_x(j, 2 * m)
                got_x(j, 2 * m + 1)

            hi, lo = split(xb[j, pl.ds(2 * m, 2)].reshape(2 * width, block))
            both = jnp.concatenate([hi, lo], axis=0)
            for t in range(3):
                at = slice(t * panel, (t + 1) * panel)
                first = dot(both, lh[4 + j, :, at])
                value = first[: 2 * width] + (first[2 * width :] + dot(hi, ll[4 + j, :, at]))
                sums[m, :, at] = jnp.where(j == 0, 0.0, sums[m, :, at]) + value
            return carry

        lax.fori_loop(0, 4, term, 0)
        send_sum(m).start()
        return carry

    def close_all():
        lax.fori_loop(0, 4, close_cross, 0)
        finish(7)

    def chunk(c, carry):
        early_x(c)

        def earlier(j, carry):
            @pl.when(j == x - 1)
            def _():
                got_x(j, c)
                update(c, j, 1)

            @pl.when(jnp.logical_and(j < x - 1, c % 2 == 0))
            def _():
                @pl.when(jnp.logical_not(early(j)))
                def _():
                    got_x(j, c)
                    got_x(j, c + 1)

                update(c, j, 2)

            return carry

        lax.fori_loop(0, x, earlier, 0)
        solve(c)

        @pl.when(jnp.logical_and(jnp.logical_and(is_a, x > 0), jnp.logical_and(c % 2 == 1, c // 2 < kept)))
        def _():
            far_on(4 + c // 2)

        @pl.when(jnp.logical_and(is_a, c >= behind))
        def _():
            @pl.when(c == behind)
            def _():
                close_all()

            @pl.when((c - behind) % 2 == 1)
            def _():
                total((c - behind) // 2, 0)

        return carry

    lax.fori_loop(0, n, chunk, 0)
    for i in range(n, n + 3):

        @pl.when(is_b)
        def _():
            early_x(i)

    @pl.when(is_a)
    def _():
        @pl.when(x == 0)
        def _():
            def pass_second(c, carry):
                got_x(1, c)
                return carry

            def far_cross_group(s, carry):
                far_on(4 + s)
                return carry

            lax.fori_loop(0, kept, pass_on_cross, 0)
            lax.fori_loop(0, kept - 1, far_cross_group, 0)
            lax.fori_loop(0, n // 2, pass_second, 0)
            lax.fori_loop(kept - 1, kept, far_cross_group, 0)

        @pl.when(x < 2)
        def _():
            close_all()

        lax.fori_loop((n - behind) // 2, n // 2, total, 0)

    def sent_ring(slot, k=3):
        for a in range(2):
            for way in range(2):
                relay(slot, yh, z, send_z.at[slot, a, way], above, k).wait_send()
        far_up(slot, k).wait_send()
        far_down(slot, k).wait_send()

    def sent_own(slot, carry):
        def corner_sent():
            relay(slot, yh, z, send_y.at[slot, z], partner, 1).wait_send()
            sent_ring(slot, 1)
            to_twin(slot, 1).wait_send()

        def along_sent():
            for z_ in range(4):
                relay(slot, yh, z, send_y.at[slot, z_], partner).wait_send()
            for way in range(2):
                relay(slot, yh, z, send_z.at[slot, yh, way], above).wait_send()
            ring_one(slot, 0).wait_send()
            to_twin(slot).wait_send()

        def plain_sent():
            relay(slot, yh, z, send_y.at[slot, z], partner).wait_send()
            sent_ring(slot)
            to_twin(slot).wait_send()

        by_kind(slot, corner_sent, along_sent, plain_sent)
        return carry

    lax.fori_loop(0, x + 1, sent_own, 0)

    @pl.when(is_a)
    def _():
        def sent_used(s, carry):
            @pl.when(s < kept)
            def _():
                sent_ring(4 + s)

            to_twin(4 + s).wait_send()
            return carry

        lax.fori_loop(0, 4, sent_used, 0)

    @pl.when(is_b)
    def _():
        def sent_cross(s, carry):
            for far in range(2):
                over_y(panels(s), s, z, far).wait_send()

            @pl.when(s >= kept)
            def _():
                for way in range(2):
                    send_shard(panels(s), 4 + s, yh, z, send_z.at[4 + s, yh, way], above).wait_send()
                far_cross(s, 0).wait_send()
                for come in (up_z, down_z, (z + 2) % 4):
                    for far in range(2):
                        over_y(panels(s), s, come, far).wait_send()

            return carry

        lax.fori_loop(0, 4, sent_cross, 0)

    def sent_x(c, carry):
        @pl.when(own_east)
        def _():
            send_own_x(c, 0).wait_send()

        @pl.when(own_west(c))
        def _():
            send_own_x(c, 1).wait_send()

        @pl.when(far_east(c))
        def _():
            forward_x(x, c, 0).wait_send()

        @pl.when(far_west(c))
        def _():
            forward_x(x, c, 1).wait_send()

        @pl.when(jnp.logical_and(is_a, c % 2 == 0))
        def _():
            send_sum(c // 2).wait_send()

        return carry

    lax.fori_loop(0, n, sent_x, 0)


def body(factor, inverses, right_side):
    n = CHUNKS
    block, cols = right_side.shape
    panel = inverses.shape[1]
    part = factor.shape[2]
    width = cols // n
    turned = jnp.transpose(factor, (1, 2, 0))
    dma = pltpu.SemaphoreType.DMA
    vmem = pl.BlockSpec(memory_space=pltpu.VMEM)
    return pl.pallas_call(
        functools.partial(kernel, n),
        out_shape=jax.ShapeDtypeStruct((block, cols), F32),
        in_specs=[pl.BlockSpec(memory_space=pl.ANY), vmem, vmem],
        out_specs=vmem,
        scratch_shapes=[
            pltpu.VMEM((8, 2, 3, 8, part, block), F32),
            pltpu.VMEM((8, block, block), BF16),
            pltpu.VMEM((8, block, block), BF16),
            pltpu.VMEM((4, n, width, block), F32),
            pltpu.VMEM((n, width, block), F32),
            pltpu.VMEM((n // 2, 2 * width, block), F32),
            pltpu.VMEM((3, panel, panel), BF16),
            pltpu.VMEM((3, panel, panel), BF16),
            dma((6,)),
            dma((4, 4)),
            dma((4, 4, 2)),
            dma((8, 2, 2)),
            dma((8, 2)),
            dma((8,)),
            dma((8, 8)),
            dma((8,)),
            dma((n, 2)),
            dma((n, 2)),
            dma((4, n)),
            dma((n,)),
            dma((n,)),
        ],
        compiler_params=pltpu.CompilerParams(
            collective_id=0, has_side_effects=True, vmem_limit_bytes=60 * 1024 * 1024
        ),
    )(turned, inverses, right_side)


def solution(mesh):
    placed = (P("row", None, "rhs"), P("row", None, None), P("row", "rhs"))
    return jax.shard_map(
        body, mesh=mesh, in_specs=placed, out_specs=P("row", "rhs"), check_vma=False
    )
```

```python
import functools

import jax
import jax.numpy as jnp
from jax import lax
from jax.experimental import pallas as pl
from jax.experimental.pallas import tpu as pltpu
from jax.sharding import PartitionSpec as P

MESH = pl.DeviceIdType.MESH
CHUNKS = 16
LEAD = 5
FAR = 6
AHEAD = 2
KEPT3 = 1
TAKE = (1, 2, 1, 0)
BEHIND2 = 8
BEHIND3 = 8
F32, BF16 = jnp.float32, jnp.bfloat16


def split(v):
    hi = v.astype(BF16)
    return hi, (v - hi.astype(F32)).astype(BF16)


def dot(a, b):
    return jnp.dot(a, b, preferred_element_type=F32)


def mult(v, wh, wl):
    hi, lo = split(v)
    m = v.shape[0]
    both = dot(jnp.concatenate([hi, lo], axis=0), wh)
    return both[:m] + (both[m:] + dot(hi, wl))


def kernel(
    n, factor, inverses, right, out,
    land, lh, ll, xb, res, sums, ih, il,
    own_sem, send_y, send_b, send_z, send_f, send_c, recv_l, recv_c,
    send_x, send_xf, recv_x, send_s, recv_s,
):
    row, rhs = lax.axis_index("row"), lax.axis_index("rhs")
    group, x = row // 4, row % 4
    yh, z, core = rhs // 8, (rhs // 2) % 4, rhs % 2
    is_a = group == 0
    is_b = group == 1
    panel = inverses.shape[1]
    block, cols = right.shape
    width = cols // n
    per = max(1, 128 // width)
    up_z, down_z = (z + 1) % 4, (z + 3) % 4
    right_x, left_x = (x + 1) % 4, (x + 3) % 4
    kept = jnp.where(x == 3, KEPT3, jnp.where(x == 0, 3, 2))

    def place(group_, x_, yh_, z_, core_):
        return (group_ * 4 + x_, (yh_ * 4 + z_) * 2 + core_)

    partner = place(group, x, 1 - yh, z, core)
    above, below = place(group, x, yh, up_z, core), place(group, x, yh, down_z, core)
    twin = place(group, x, yh, z, 1 - core)
    east, west = place(group, right_x, yh, z, core), place(group, left_x, yh, z, core)
    cross = place(1 - group, x, yh, z, core)
    cross_far = place(1 - group, x, 1 - yh, z, core)

    def remote(src, dst, send, recv, device):
        return pltpu.make_async_remote_copy(
            src_ref=src, dst_ref=dst, send_sem=send, recv_sem=recv, device_id=device, device_id_type=MESH
        )

    def shard(slot, yh_, z_, k=3):
        return land.at[slot, core, pl.ds(0, k), yh_ * 4 + z_]

    def panels(index):
        return factor.at[pl.ds(3 * index, 3)]

    def send_shard(src, slot, yh_, z_, send, device, k=3):
        return remote(src, shard(slot, yh_, z_, k), send, recv_l.at[slot, yh_ * 4 + z_], device)

    def got_shard(slot, yh_, z_, k=3):
        send_shard(shard(slot, yh_, z_, k), slot, yh_, z_, send_c.at[0], partner, k).wait_recv()

    def relay(slot, yh_, z_, send, device, k=3):
        return send_shard(shard(slot, yh_, z_, k), slot, yh_, z_, send, device, k)

    def own_copy(slot):
        return pltpu.make_async_copy(panels(4 * group + slot), shard(slot, yh, z), own_sem.at[slot])

    def corner(k):
        first = 3 * (4 * group + x)
        here = land.at[x, core, 0, yh * 4 + z]
        if k == 0:
            src, dst = factor.at[first, :, pl.ds(panel, 2 * panel)], here.at[:, pl.ds(panel, 2 * panel)]
        else:
            src, dst = factor.at[first + 1, :, pl.ds(2 * panel, panel)], here.at[:, pl.ds(0, panel)]
        return pltpu.make_async_copy(src, dst, own_sem.at[4 + k])

    def open_own(slot, carry):
        src = panels(4 * group + slot)
        send_shard(src, slot, yh, z, send_y.at[slot, z], partner).start()
        send_shard(src, slot, yh, z, send_z.at[slot, yh, 0], above).start()
        send_shard(src, slot, yh, z, send_z.at[slot, yh, 1], below).start()
        own_copy(slot).start()
        return carry

    def open_corner():
        corner(0).wait()
        corner(1).wait()
        relay(x, yh, z, send_y.at[x, z], partner, 1).start()
        relay(x, yh, z, send_z.at[x, yh, 0], above, 1).start()
        relay(x, yh, z, send_z.at[x, yh, 1], below, 1).start()

    def along_first(slot):
        return jnp.logical_and(jnp.logical_and(slot >= 1, slot <= 2), slot < x)

    def ring_one(slot, way):
        came, to = ((down_z, above), (up_z, below))[way]
        return relay(slot, yh, came, send_f.at[slot, 0], to)

    def along_near(slot):
        for way, came in ((0, down_z), (1, up_z)):
            got_shard(slot, yh, came)

            @pl.when(slot % 2 == way)
            def _():
                ring_one(slot, way).start()

            relay(slot, yh, came, send_y.at[slot, came], partner).start()

    def along_last(slot):
        came = (z + 2) % 4
        got_shard(slot, yh, came)
        relay(slot, yh, came, send_y.at[slot, came], partner).start()

    corner(0).start()
    corner(1).start()
    barrier = pltpu.get_barrier_semaphore()
    for device in (partner, above, below, twin, east, west, cross, cross_far):
        pl.semaphore_signal(barrier, inc=1, device_id=device, device_id_type=MESH)
    pl.semaphore_wait(barrier, 8)

    def over_y(src, s, z_, far):
        return send_shard(src, 4 + s, yh, z_, send_b.at[s, z_, far], (cross, cross_far)[far])

    def open_cross(s, carry):
        over_y(panels(s), s, z, 0).start()
        over_y(panels(s), s, z, 1).start()

        @pl.when(s >= kept)
        def _():
            send_shard(panels(s), 4 + s, yh, z, send_z.at[4 + s, yh, 0], above).start()
            send_shard(panels(s), 4 + s, yh, z, send_z.at[4 + s, yh, 1], below).start()

        return carry

    def far_cross(s, way):
        came, to = ((down_z, above), (up_z, below))[way]
        return send_shard(shard(4 + s, yh, came), 4 + s, yh, came, send_f.at[4 + s, 0], to)

    def cross_near(s, carry):
        for way, came in ((0, down_z), (1, up_z)):
            got_shard(4 + s, yh, came)

            @pl.when(s % 2 == way)
            def _():
                far_cross(s, way).start()

            for far in range(2):
                over_y(shard(4 + s, yh, came), s, came, far).start()
        return carry

    def cross_last(s, carry):
        came = (z + 2) % 4
        got_shard(4 + s, yh, came)
        for far in range(2):
            over_y(shard(4 + s, yh, came), s, came, far).start()
        return carry

    @pl.when(is_b)
    def _():
        lax.fori_loop(0, 4, open_cross, 0)

    lax.fori_loop(0, x, open_own, 0)
    open_corner()

    def pass_on(slot, yh_, k=3):
        got_shard(slot, yh_, z, k)
        relay(slot, yh_, z, send_z.at[slot, yh_, 0], above, k).start()
        relay(slot, yh_, z, send_z.at[slot, yh_, 1], below, k).start()

    def far_up(slot, k=3):
        return relay(slot, yh, down_z, send_f.at[slot, 0], above, k)

    def far_down(slot, k=3):
        return relay(slot, 1 - yh, up_z, send_f.at[slot, 1], below, k)

    def to_twin(slot, k=3):
        part = land.at[slot, core, pl.ds(0, k)]
        return remote(part, part, send_c.at[slot], recv_c.at[slot], twin)

    def halves(slot, k=3):
        def piece(i, carry):
            p, yz = i // 8, i % 8
            for c in range(2):
                hi, lo = split(land[slot, c, p, yz])
                rows = hi.shape[0]
                at = pl.ds(pl.multiple_of((i * 2 + c) * rows, rows), rows)
                lh[slot, at, :] = hi
                ll[slot, at, :] = lo
            return carry

        lax.fori_loop(0, 8 * k, piece, 0)

    def far_on(slot, k=3):
        got_shard(slot, yh, down_z, k)
        far_up(slot, k).start()
        got_shard(slot, 1 - yh, up_z, k)
        far_down(slot, k).start()

    def far_here(slot, k=3):
        got_shard(slot, 1 - yh, down_z, k)
        got_shard(slot, yh, up_z, k)
        got_shard(slot, yh, (z + 2) % 4, k)
        got_shard(slot, 1 - yh, (z + 2) % 4, k)

    def finish(slot, k=3):
        part = land.at[slot, 1 - core, pl.ds(0, k)]
        remote(part, part, send_c.at[slot], recv_c.at[slot], twin).wait_recv()
        halves(slot, k)

    def pass_on_cross(s, carry):
        pass_on(4 + s, 0)
        pass_on(4 + s, 1)
        return carry

    def close_cross(s, carry):
        @pl.when(x == 0)
        def _():
            for k in range(n // 8):
                got_x(1, n // 2 + s * (n // 8) + k)

        @pl.when(s >= kept)
        def _():
            got_shard(4 + s, yh, z)
            got_shard(4 + s, 1 - yh, z)
            got_shard(4 + s, yh, down_z)
            got_shard(4 + s, 1 - yh, up_z)

        far_here(4 + s)
        to_twin(4 + s).start()

        @pl.when(s > 0)
        def _():
            finish(3 + s)

        return carry

    def send_own_x(c, way):
        device = (east, west)[way]
        return remote(xb.at[x, c], xb.at[x, c], send_x.at[c, way], recv_x.at[x, c], device)

    own_east = jnp.logical_or(is_a, x < 3)

    def own_west(c):
        return jnp.logical_or(is_a, jnp.logical_or(x == 0, jnp.logical_and(x == 1, c % 2 == 1)))

    def far_east(c):
        on_a = jnp.logical_or(jnp.logical_or(x == 0, jnp.logical_and(x == 3, c % 2 == 0)), jnp.logical_or(jnp.logical_and(x == 2, c < 2), jnp.logical_and(x == 1, c >= 8)))
        on_b = jnp.logical_and(x == 2, c % 2 == 0)
        return jnp.logical_or(jnp.logical_and(is_a, on_a), jnp.logical_and(is_b, on_b))

    def far_west(c):
        on_a = jnp.logical_or(jnp.logical_and(x == 1, c % 2 == 1), jnp.logical_and(x == 0, c >= 2))
        on_b = jnp.logical_and(x == 0, c % 2 == 1)
        either = jnp.logical_or(jnp.logical_and(is_a, on_a), jnp.logical_and(is_b, on_b))
        return jnp.logical_or(jnp.logical_and(x == 3, jnp.logical_or(is_b, c < 8)), either)

    def forward_x(j, c, way):
        return remote(xb.at[j, c], xb.at[j, c], send_xf.at[c, way], recv_x.at[j, c], (east, west)[way])

    def got_x(j, c):
        remote(xb.at[j, c], xb.at[j, c], send_x.at[c, 0], recv_x.at[j, c], east).wait_recv()

        @pl.when(jnp.logical_and(j == left_x, far_east(c)))
        def _():
            forward_x(j, c, 0).start()

        @pl.when(jnp.logical_and(j == right_x, far_west(c)))
        def _():
            forward_x(j, c, 1).start()

    unit = max(1, n // 8)
    taken = sum(TAKE) * unit

    def early_group(v):
        @pl.when(jnp.logical_and(is_a, x == 3))
        def _():
            for at, take in enumerate(TAKE):
                first = sum(TAKE[:at]) * unit

                @pl.when(v == at)
                def _(first=first, take=take):
                    for k in range(take * unit):
                        got_x(0, first + k)

    def early_x(i):
        @pl.when(jnp.logical_and(jnp.logical_and(is_b, x == 3), i + LEAD < n))
        def _():
            @pl.when(i == 0)
            def _():
                for k in range(LEAD):
                    got_x(0, k)

            got_x(0, i + LEAD)

        @pl.when(jnp.logical_and(jnp.logical_and(is_a, x == 3), i + taken < n))
        def _():
            got_x(0, i + taken)

        @pl.when(jnp.logical_and(jnp.logical_and(is_b, x == 0), jnp.logical_and(i >= 3, i % 2 == 0)))
        def _():
            got_x(1, i - 3)

        @pl.when(jnp.logical_and(jnp.logical_and(is_a, x == 1), i >= n - AHEAD))
        def _():
            got_x(2, i - (n - AHEAD))

    def early(j):
        return jnp.logical_and(x == 3, j == 0)

    def send_sum(c):
        return remote(sums.at[c], sums.at[c], send_s.at[c], recv_s.at[c], cross)

    def update(c, j, m):
        hi, lo = split(xb[j, pl.ds(c, m)].reshape(m * width, block))
        both = jnp.concatenate([hi, lo], axis=0)
        for t in range(3):
            at = slice(t * panel, (t + 1) * panel)
            first = dot(both, lh[j, :, at])
            value = first[: m * width] + (first[m * width :] + dot(hi, ll[j, :, at]))
            res[pl.ds(c, m), :, at] -= value.reshape(m, width, panel)

    def solve(c):
        @pl.when(is_b)
        def _():
            @pl.when(c % 2 == 0)
            def _():
                send_sum(c // 2).wait_recv()

            res[c] = res[c] - sums[c // 2, pl.ds(pl.multiple_of(c % 2 * width, width), width)]

        one, two = slice(panel, 2 * panel), slice(2 * panel, 3 * panel)
        x0 = mult(res[c, :, :panel], ih[0], il[0])
        xb[x, c, :, :panel] = x0
        rest = res[c, :, panel:] - mult(x0, lh[x, :panel, panel:], ll[x, :panel, panel:])
        x1 = mult(rest[:, :panel], ih[1], il[1])
        xb[x, c, :, one] = x1
        last = rest[:, panel:] - mult(x1, lh[x, :panel, :panel], ll[x, :panel, :panel])
        xb[x, c, :, two] = mult(last, ih[2], il[2])

        @pl.when(own_east)
        def _():
            send_own_x(c, 0).start()

        @pl.when(own_west(c))
        def _():
            send_own_x(c, 1).start()

        @pl.when(c % per == per - 1)
        def _():
            both = xb[x, pl.ds(c - (per - 1), per)].reshape(per * width, block)
            out[:, pl.ds(pl.multiple_of((c // per) * per * width, per * width), per * width)] = both.T

    for p in range(3):
        hi, lo = split(inverses[p].T)
        ih[p] = hi
        il[p] = lo

    def flip(i, carry):
        turned = right[:, pl.ds(pl.multiple_of(i * per * width, per * width), per * width)].T
        res[pl.ds(i * per, per)] = turned.reshape(per, width, block)
        return carry

    lax.fori_loop(0, n // per, flip, 0)

    @pl.when(is_b)
    def _():
        lax.fori_loop(kept, 4, cross_near, 0)
        lax.fori_loop(kept, 4, cross_last, 0)

    def by_kind(slot, on_corner, on_along, on_plain):
        @pl.when(slot == x)
        def _():
            on_corner()

        @pl.when(slot < x)
        def _():
            along = along_first(slot)

            @pl.when(along)
            def _():
                on_along()

            @pl.when(jnp.logical_not(along))
            def _():
                on_plain()

    def own_near(u):
        by_kind(u, lambda: pass_on(u, 1 - yh, 1), lambda: along_near(u), lambda: pass_on(u, 1 - yh))

    def own_far(u):
        by_kind(u, lambda: far_on(u, 1), lambda: along_last(u), lambda: far_on(u))

    def own_all(u):
        def corner_all():
            far_here(u, 1)
            to_twin(u, 1).start()

        def along_all():
            own_copy(u).wait()
            for z_ in range(4):
                got_shard(u, 1 - yh, z_)
            to_twin(u).start()

        def plain_all():
            own_copy(u).wait()
            far_here(u)
            to_twin(u).start()

        by_kind(u, corner_all, along_all, plain_all)

    def own_group(v, carry):
        own_all(v)

        @pl.when(v > 0)
        def _():
            finish(v - 1)

        early_group(v)
        return carry

    def near_group(u, carry):
        own_near(u)
        return carry

    def far_group(u, carry):
        own_far(u)
        return carry

    lax.fori_loop(0, x + 1, near_group, 0)
    lax.fori_loop(0, x + 1, far_group, 0)

    @pl.when(jnp.logical_and(is_a, x > 0))
    def _():
        lax.fori_loop(0, kept, pass_on_cross, 0)

    lax.fori_loop(0, x + 1, own_group, 0)
    finish(x, 1)

    ahead = jnp.where(x == 1, AHEAD, 0)
    behind = jnp.where(x == 3, BEHIND3, jnp.where(x == 2, BEHIND2, n))

    def total(m, carry):
        for k in range(2):

            @pl.when(jnp.logical_and(x == 1, 2 * m + k + ahead < n))
            def _(k=k):
                got_x(x + 1, 2 * m + k + ahead)

        def term(j, carry):
            @pl.when(jnp.logical_and(j > x, jnp.logical_or(x >= 2, j > x + 1)))
            def _():
                got_x(j, 2 * m)
                got_x(j, 2 * m + 1)

            hi, lo = split(xb[j, pl.ds(2 * m, 2)].reshape(2 * width, block))
            both = jnp.concatenate([hi, lo], axis=0)
            for t in range(3):
                at = slice(t * panel, (t + 1) * panel)
                first = dot(both, lh[4 + j, :, at])
                value = first[: 2 * width] + (first[2 * width :] + dot(hi, ll[4 + j, :, at]))
                sums[m, :, at] = jnp.where(j == 0, 0.0, sums[m, :, at]) + value
            return carry

        lax.fori_loop(0, 4, term, 0)
        send_sum(m).start()
        return carry

    def close_all():
        lax.fori_loop(0, 4, close_cross, 0)
        finish(7)

    def chunk(c, carry):
        early_x(c)

        def earlier(j, carry):
            @pl.when(j == x - 1)
            def _():
                got_x(j, c)
                update(c, j, 1)

            @pl.when(jnp.logical_and(j < x - 1, c % 2 == 0))
            def _():
                @pl.when(jnp.logical_not(early(j)))
                def _():
                    got_x(j, c)
                    got_x(j, c + 1)

                update(c, j, 2)

            return carry

        lax.fori_loop(0, x, earlier, 0)
        solve(c)

        @pl.when(jnp.logical_and(jnp.logical_and(is_a, x > 0), jnp.logical_and(c >= FAR, c - FAR < kept)))
        def _():
            far_on(4 + c - FAR)

        @pl.when(jnp.logical_and(is_a, c >= behind))
        def _():
            @pl.when(c == behind)
            def _():
                close_all()

            @pl.when((c - behind) % 2 == 1)
            def _():
                total((c - behind) // 2, 0)

        return carry

    lax.fori_loop(0, n, chunk, 0)
    for i in range(n, n + 3):

        @pl.when(is_b)
        def _():
            early_x(i)

    @pl.when(is_a)
    def _():
        @pl.when(x == 0)
        def _():
            def pass_second(c, carry):
                got_x(1, c)
                return carry

            def far_cross_group(s, carry):
                far_on(4 + s)
                return carry

            lax.fori_loop(0, kept, pass_on_cross, 0)
            lax.fori_loop(0, kept - 1, far_cross_group, 0)
            lax.fori_loop(0, n // 2, pass_second, 0)
            lax.fori_loop(kept - 1, kept, far_cross_group, 0)

        @pl.when(behind == n)
        def _():
            close_all()

        lax.fori_loop((n - behind) // 2, n // 2, total, 0)

    def sent_ring(slot, k=3):
        for a in range(2):
            for way in range(2):
                relay(slot, yh, z, send_z.at[slot, a, way], above, k).wait_send()
        far_up(slot, k).wait_send()
        far_down(slot, k).wait_send()

    def sent_own(slot, carry):
        def corner_sent():
            relay(slot, yh, z, send_y.at[slot, z], partner, 1).wait_send()
            sent_ring(slot, 1)
            to_twin(slot, 1).wait_send()

        def along_sent():
            for z_ in range(4):
                relay(slot, yh, z, send_y.at[slot, z_], partner).wait_send()
            for way in range(2):
                relay(slot, yh, z, send_z.at[slot, yh, way], above).wait_send()
            ring_one(slot, 0).wait_send()
            to_twin(slot).wait_send()

        def plain_sent():
            relay(slot, yh, z, send_y.at[slot, z], partner).wait_send()
            sent_ring(slot)
            to_twin(slot).wait_send()

        by_kind(slot, corner_sent, along_sent, plain_sent)
        return carry

    lax.fori_loop(0, x + 1, sent_own, 0)

    @pl.when(is_a)
    def _():
        def sent_used(s, carry):
            @pl.when(s < kept)
            def _():
                sent_ring(4 + s)

            to_twin(4 + s).wait_send()
            return carry

        lax.fori_loop(0, 4, sent_used, 0)

    @pl.when(is_b)
    def _():
        def sent_cross(s, carry):
            for far in range(2):
                over_y(panels(s), s, z, far).wait_send()

            @pl.when(s >= kept)
            def _():
                for way in range(2):
                    send_shard(panels(s), 4 + s, yh, z, send_z.at[4 + s, yh, way], above).wait_send()
                far_cross(s, 0).wait_send()
                for come in (up_z, down_z, (z + 2) % 4):
                    for far in range(2):
                        over_y(panels(s), s, come, far).wait_send()

            return carry

        lax.fori_loop(0, 4, sent_cross, 0)

    def sent_x(c, carry):
        @pl.when(own_east)
        def _():
            send_own_x(c, 0).wait_send()

        @pl.when(own_west(c))
        def _():
            send_own_x(c, 1).wait_send()

        @pl.when(far_east(c))
        def _():
            forward_x(x, c, 0).wait_send()

        @pl.when(far_west(c))
        def _():
            forward_x(x, c, 1).wait_send()

        @pl.when(jnp.logical_and(is_a, c % 2 == 0))
        def _():
            send_sum(c // 2).wait_send()

        return carry

    lax.fori_loop(0, n, sent_x, 0)


def body(factor, inverses, right_side):
    n = CHUNKS
    block, cols = right_side.shape
    panel = inverses.shape[1]
    part = factor.shape[2]
    width = cols // n
    turned = jnp.transpose(factor, (1, 2, 0))
    dma = pltpu.SemaphoreType.DMA
    vmem = pl.BlockSpec(memory_space=pltpu.VMEM)
    return pl.pallas_call(
        functools.partial(kernel, n),
        out_shape=jax.ShapeDtypeStruct((block, cols), F32),
        in_specs=[pl.BlockSpec(memory_space=pl.ANY), vmem, vmem],
        out_specs=vmem,
        scratch_shapes=[
            pltpu.VMEM((8, 2, 3, 8, part, block), F32),
            pltpu.VMEM((8, block, block), BF16),
            pltpu.VMEM((8, block, block), BF16),
            pltpu.VMEM((4, n, width, block), F32),
            pltpu.VMEM((n, width, block), F32),
            pltpu.VMEM((n // 2, 2 * width, block), F32),
            pltpu.VMEM((3, panel, panel), BF16),
            pltpu.VMEM((3, panel, panel), BF16),
            dma((6,)),
            dma((4, 4)),
            dma((4, 4, 2)),
            dma((8, 2, 2)),
            dma((8, 2)),
            dma((8,)),
            dma((8, 8)),
            dma((8,)),
            dma((n, 2)),
            dma((n, 2)),
            dma((4, n)),
            dma((n,)),
            dma((n,)),
        ],
        compiler_params=pltpu.CompilerParams(
            collective_id=0, has_side_effects=True, vmem_limit_bytes=60 * 1024 * 1024
        ),
    )(turned, inverses, right_side)


def solution(mesh):
    placed = (P("row", None, "rhs"), P("row", None, None), P("row", "rhs"))
    return jax.shard_map(
        body, mesh=mesh, in_specs=placed, out_specs=P("row", "rhs"), check_vma=False
    )
```

```python
import functools

import jax
import jax.numpy as jnp
from jax import lax
from jax.experimental import pallas as pl
from jax.experimental.pallas import tpu as pltpu
from jax.sharding import PartitionSpec as P

MESH = pl.DeviceIdType.MESH
CHUNKS = 16
LEAD = 4
FAR = 6
AHEAD = 2
KEPT3 = 1
TAKE = (1, 2, 1, 0)
BEHIND2 = 8
BEHIND3 = 8
F32, BF16 = jnp.float32, jnp.bfloat16


def split(v):
    hi = v.astype(BF16)
    return hi, (v - hi.astype(F32)).astype(BF16)


def dot(a, b):
    return jnp.dot(a, b, preferred_element_type=F32)


def mult(v, wh, wl):
    hi, lo = split(v)
    m = v.shape[0]
    both = dot(jnp.concatenate([hi, lo], axis=0), wh)
    return both[:m] + (both[m:] + dot(hi, wl))


def kernel(
    n, factor, inverses, right, out,
    land, lh, ll, xb, res, sums, ih, il,
    own_sem, send_y, send_b, send_z, send_f, send_c, recv_l, recv_c,
    send_x, send_xf, recv_x, send_s, recv_s,
):
    row, rhs = lax.axis_index("row"), lax.axis_index("rhs")
    group, x = row // 4, row % 4
    yh, z, core = rhs // 8, (rhs // 2) % 4, rhs % 2
    is_a = group == 0
    is_b = group == 1
    panel = inverses.shape[1]
    block, cols = right.shape
    width = cols // n
    per = max(1, 128 // width)
    up_z, down_z = (z + 1) % 4, (z + 3) % 4
    right_x, left_x = (x + 1) % 4, (x + 3) % 4
    kept = jnp.where(x == 3, KEPT3, jnp.where(x == 0, 3, 2))

    def place(group_, x_, yh_, z_, core_):
        return (group_ * 4 + x_, (yh_ * 4 + z_) * 2 + core_)

    partner = place(group, x, 1 - yh, z, core)
    above, below = place(group, x, yh, up_z, core), place(group, x, yh, down_z, core)
    twin = place(group, x, yh, z, 1 - core)
    east, west = place(group, right_x, yh, z, core), place(group, left_x, yh, z, core)
    cross = place(1 - group, x, yh, z, core)
    cross_far = place(1 - group, x, 1 - yh, z, core)

    def remote(src, dst, send, recv, device):
        return pltpu.make_async_remote_copy(
            src_ref=src, dst_ref=dst, send_sem=send, recv_sem=recv, device_id=device, device_id_type=MESH
        )

    def shard(slot, yh_, z_, k=3):
        return land.at[slot, core, pl.ds(0, k), yh_ * 4 + z_]

    def panels(index):
        return factor.at[pl.ds(3 * index, 3)]

    def send_shard(src, slot, yh_, z_, send, device, k=3):
        return remote(src, shard(slot, yh_, z_, k), send, recv_l.at[slot, yh_ * 4 + z_], device)

    def got_shard(slot, yh_, z_, k=3):
        send_shard(shard(slot, yh_, z_, k), slot, yh_, z_, send_c.at[0], partner, k).wait_recv()

    def relay(slot, yh_, z_, send, device, k=3):
        return send_shard(shard(slot, yh_, z_, k), slot, yh_, z_, send, device, k)

    def own_copy(slot):
        return pltpu.make_async_copy(panels(4 * group + slot), shard(slot, yh, z), own_sem.at[slot])

    def corner(k):
        first = 3 * (4 * group + x)
        here = land.at[x, core, 0, yh * 4 + z]
        if k == 0:
            src, dst = factor.at[first, :, pl.ds(panel, 2 * panel)], here.at[:, pl.ds(panel, 2 * panel)]
        else:
            src, dst = factor.at[first + 1, :, pl.ds(2 * panel, panel)], here.at[:, pl.ds(0, panel)]
        return pltpu.make_async_copy(src, dst, own_sem.at[4 + k])

    def open_own(slot, carry):
        src = panels(4 * group + slot)
        send_shard(src, slot, yh, z, send_y.at[slot, z], partner).start()
        send_shard(src, slot, yh, z, send_z.at[slot, yh, 0], above).start()
        send_shard(src, slot, yh, z, send_z.at[slot, yh, 1], below).start()
        own_copy(slot).start()
        return carry

    def open_corner():
        corner(0).wait()
        corner(1).wait()
        relay(x, yh, z, send_y.at[x, z], partner, 1).start()
        relay(x, yh, z, send_z.at[x, yh, 0], above, 1).start()
        relay(x, yh, z, send_z.at[x, yh, 1], below, 1).start()

    def along_first(slot):
        return jnp.logical_and(jnp.logical_and(slot >= 1, slot <= 2), slot < x)

    def ring_one(slot, way):
        came, to = ((down_z, above), (up_z, below))[way]
        return relay(slot, yh, came, send_f.at[slot, 0], to)

    def along_near(slot):
        for way, came in ((0, down_z), (1, up_z)):
            got_shard(slot, yh, came)

            @pl.when(slot % 2 == way)
            def _():
                ring_one(slot, way).start()

            relay(slot, yh, came, send_y.at[slot, came], partner).start()

    def along_last(slot):
        came = (z + 2) % 4
        got_shard(slot, yh, came)
        relay(slot, yh, came, send_y.at[slot, came], partner).start()

    corner(0).start()
    corner(1).start()
    barrier = pltpu.get_barrier_semaphore()
    for device in (partner, above, below, twin, east, west, cross, cross_far):
        pl.semaphore_signal(barrier, inc=1, device_id=device, device_id_type=MESH)
    pl.semaphore_wait(barrier, 8)

    def over_y(src, s, z_, far):
        return send_shard(src, 4 + s, yh, z_, send_b.at[s, z_, far], (cross, cross_far)[far])

    def open_cross(s, carry):
        over_y(panels(s), s, z, 0).start()
        over_y(panels(s), s, z, 1).start()

        @pl.when(s >= kept)
        def _():
            send_shard(panels(s), 4 + s, yh, z, send_z.at[4 + s, yh, 0], above).start()
            send_shard(panels(s), 4 + s, yh, z, send_z.at[4 + s, yh, 1], below).start()

        return carry

    def far_cross(s, way):
        came, to = ((down_z, above), (up_z, below))[way]
        return send_shard(shard(4 + s, yh, came), 4 + s, yh, came, send_f.at[4 + s, 0], to)

    def cross_near(s, carry):
        for way, came in ((0, down_z), (1, up_z)):
            got_shard(4 + s, yh, came)

            @pl.when(s % 2 == way)
            def _():
                far_cross(s, way).start()

            for far in range(2):
                over_y(shard(4 + s, yh, came), s, came, far).start()
        return carry

    def cross_last(s, carry):
        came = (z + 2) % 4
        got_shard(4 + s, yh, came)
        for far in range(2):
            over_y(shard(4 + s, yh, came), s, came, far).start()
        return carry

    @pl.when(is_b)
    def _():
        lax.fori_loop(0, 4, open_cross, 0)

    lax.fori_loop(0, x, open_own, 0)
    open_corner()

    def pass_on(slot, yh_, k=3):
        got_shard(slot, yh_, z, k)
        relay(slot, yh_, z, send_z.at[slot, yh_, 0], above, k).start()
        relay(slot, yh_, z, send_z.at[slot, yh_, 1], below, k).start()

    def far_up(slot, k=3):
        return relay(slot, yh, down_z, send_f.at[slot, 0], above, k)

    def far_down(slot, k=3):
        return relay(slot, 1 - yh, up_z, send_f.at[slot, 1], below, k)

    def to_twin(slot, k=3):
        part = land.at[slot, core, pl.ds(0, k)]
        return remote(part, part, send_c.at[slot], recv_c.at[slot], twin)

    def halves(slot, k=3):
        def piece(i, carry):
            p, yz = i // 8, i % 8
            for c in range(2):
                hi, lo = split(land[slot, c, p, yz])
                rows = hi.shape[0]
                at = pl.ds(pl.multiple_of((i * 2 + c) * rows, rows), rows)
                lh[slot, at, :] = hi
                ll[slot, at, :] = lo
            return carry

        lax.fori_loop(0, 8 * k, piece, 0)

    def far_on(slot, k=3):
        got_shard(slot, yh, down_z, k)
        far_up(slot, k).start()
        got_shard(slot, 1 - yh, up_z, k)
        far_down(slot, k).start()

    def far_here(slot, k=3):
        got_shard(slot, 1 - yh, down_z, k)
        got_shard(slot, yh, up_z, k)
        got_shard(slot, yh, (z + 2) % 4, k)
        got_shard(slot, 1 - yh, (z + 2) % 4, k)

    def finish(slot, k=3):
        part = land.at[slot, 1 - core, pl.ds(0, k)]
        remote(part, part, send_c.at[slot], recv_c.at[slot], twin).wait_recv()
        halves(slot, k)

    def pass_on_cross(s, carry):
        pass_on(4 + s, 0)
        pass_on(4 + s, 1)
        return carry

    def close_cross(s, carry):
        @pl.when(x == 0)
        def _():
            for k in range(n // 8):
                got_x(1, n // 2 + s * (n // 8) + k)

        @pl.when(s >= kept)
        def _():
            got_shard(4 + s, yh, z)
            got_shard(4 + s, 1 - yh, z)
            got_shard(4 + s, yh, down_z)
            got_shard(4 + s, 1 - yh, up_z)

        far_here(4 + s)
        to_twin(4 + s).start()

        @pl.when(s > 0)
        def _():
            finish(3 + s)

        return carry

    def send_own_x(c, way):
        device = (east, west)[way]
        return remote(xb.at[x, c], xb.at[x, c], send_x.at[c, way], recv_x.at[x, c], device)

    own_east = jnp.logical_or(is_a, x < 3)

    def own_west(c):
        return jnp.logical_or(is_a, jnp.logical_or(x == 0, jnp.logical_and(x == 1, c % 2 == 1)))

    def far_east(c):
        on_a = jnp.logical_or(jnp.logical_or(x == 0, jnp.logical_and(x == 3, c % 2 == 0)), jnp.logical_or(jnp.logical_and(x == 2, c < 2), jnp.logical_and(x == 1, c >= 8)))
        on_b = jnp.logical_and(x == 2, c % 2 == 0)
        return jnp.logical_or(jnp.logical_and(is_a, on_a), jnp.logical_and(is_b, on_b))

    def far_west(c):
        on_a = jnp.logical_or(jnp.logical_and(x == 1, c % 2 == 1), jnp.logical_and(x == 0, c >= 2))
        on_b = jnp.logical_and(x == 0, c % 2 == 1)
        either = jnp.logical_or(jnp.logical_and(is_a, on_a), jnp.logical_and(is_b, on_b))
        return jnp.logical_or(jnp.logical_and(x == 3, jnp.logical_or(is_b, c < 8)), either)

    def forward_x(j, c, way):
        return remote(xb.at[j, c], xb.at[j, c], send_xf.at[c, way], recv_x.at[j, c], (east, west)[way])

    def got_x(j, c):
        remote(xb.at[j, c], xb.at[j, c], send_x.at[c, 0], recv_x.at[j, c], east).wait_recv()

        @pl.when(jnp.logical_and(j == left_x, far_east(c)))
        def _():
            forward_x(j, c, 0).start()

        @pl.when(jnp.logical_and(j == right_x, far_west(c)))
        def _():
            forward_x(j, c, 1).start()

    unit = max(1, n // 8)
    taken = sum(TAKE) * unit

    def early_group(v):
        @pl.when(jnp.logical_and(is_a, x == 3))
        def _():
            for at, take in enumerate(TAKE):
                first = sum(TAKE[:at]) * unit

                @pl.when(v == at)
                def _(first=first, take=take):
                    for k in range(take * unit):
                        got_x(0, first + k)

    def early_x(i):
        @pl.when(jnp.logical_and(jnp.logical_and(is_b, x == 3), i + LEAD < n))
        def _():
            @pl.when(i == 0)
            def _():
                for k in range(LEAD):
                    got_x(0, k)

            got_x(0, i + LEAD)

        @pl.when(jnp.logical_and(jnp.logical_and(is_a, x == 3), i + taken < n))
        def _():
            got_x(0, i + taken)

        @pl.when(jnp.logical_and(jnp.logical_and(is_b, x == 0), jnp.logical_and(i >= 3, i % 2 == 0)))
        def _():
            got_x(1, i - 3)

        @pl.when(jnp.logical_and(jnp.logical_and(is_a, x == 1), i >= n - AHEAD))
        def _():
            got_x(2, i - (n - AHEAD))

    def early(j):
        return jnp.logical_and(x == 3, j == 0)

    def send_sum(c):
        return remote(sums.at[c], sums.at[c], send_s.at[c], recv_s.at[c], cross)

    def update(c, j, m):
        hi, lo = split(xb[j, pl.ds(c, m)].reshape(m * width, block))
        both = jnp.concatenate([hi, lo], axis=0)
        for t in range(3):
            at = slice(t * panel, (t + 1) * panel)
            first = dot(both, lh[j, :, at])
            value = first[: m * width] + (first[m * width :] + dot(hi, ll[j, :, at]))
            res[pl.ds(c, m), :, at] -= value.reshape(m, width, panel)

    def solve(c):
        @pl.when(is_b)
        def _():
            @pl.when(c % 2 == 0)
            def _():
                send_sum(c // 2).wait_recv()

            res[c] = res[c] - sums[c // 2, pl.ds(pl.multiple_of(c % 2 * width, width), width)]

        one, two = slice(panel, 2 * panel), slice(2 * panel, 3 * panel)
        x0 = mult(res[c, :, :panel], ih[0], il[0])
        xb[x, c, :, :panel] = x0
        rest = res[c, :, panel:] - mult(x0, lh[x, :panel, panel:], ll[x, :panel, panel:])
        x1 = mult(rest[:, :panel], ih[1], il[1])
        xb[x, c, :, one] = x1
        last = rest[:, panel:] - mult(x1, lh[x, :panel, :panel], ll[x, :panel, :panel])
        xb[x, c, :, two] = mult(last, ih[2], il[2])

        @pl.when(own_east)
        def _():
            send_own_x(c, 0).start()

        @pl.when(own_west(c))
        def _():
            send_own_x(c, 1).start()

        @pl.when(c % per == per - 1)
        def _():
            both = xb[x, pl.ds(c - (per - 1), per)].reshape(per * width, block)
            out[:, pl.ds(pl.multiple_of((c // per) * per * width, per * width), per * width)] = both.T

    for p in range(3):
        hi, lo = split(inverses[p].T)
        ih[p] = hi
        il[p] = lo

    def flip(i, carry):
        turned = right[:, pl.ds(pl.multiple_of(i * per * width, per * width), per * width)].T
        res[pl.ds(i * per, per)] = turned.reshape(per, width, block)
        return carry

    lax.fori_loop(0, n // per, flip, 0)

    @pl.when(is_b)
    def _():
        lax.fori_loop(kept, 4, cross_near, 0)
        lax.fori_loop(kept, 4, cross_last, 0)

    def by_kind(slot, on_corner, on_along, on_plain):
        @pl.when(slot == x)
        def _():
            on_corner()

        @pl.when(slot < x)
        def _():
            along = along_first(slot)

            @pl.when(along)
            def _():
                on_along()

            @pl.when(jnp.logical_not(along))
            def _():
                on_plain()

    def own_near(u):
        by_kind(u, lambda: pass_on(u, 1 - yh, 1), lambda: along_near(u), lambda: pass_on(u, 1 - yh))

    def own_far(u):
        by_kind(u, lambda: far_on(u, 1), lambda: along_last(u), lambda: far_on(u))

    def own_all(u):
        def corner_all():
            far_here(u, 1)
            to_twin(u, 1).start()

        def along_all():
            own_copy(u).wait()
            for z_ in range(4):
                got_shard(u, 1 - yh, z_)
            to_twin(u).start()

        def plain_all():
            own_copy(u).wait()
            far_here(u)
            to_twin(u).start()

        by_kind(u, corner_all, along_all, plain_all)

    def own_group(v, carry):
        own_all(v)

        @pl.when(v > 0)
        def _():
            finish(v - 1)

        early_group(v)
        return carry

    def near_group(u, carry):
        own_near(u)
        return carry

    def far_group(u, carry):
        own_far(u)
        return carry

    lax.fori_loop(0, x + 1, near_group, 0)
    lax.fori_loop(0, x + 1, far_group, 0)

    @pl.when(jnp.logical_and(is_a, x > 0))
    def _():
        lax.fori_loop(0, kept, pass_on_cross, 0)

    lax.fori_loop(0, x + 1, own_group, 0)
    finish(x, 1)

    ahead = jnp.where(x == 1, AHEAD, 0)
    behind = jnp.where(x == 3, BEHIND3, jnp.where(x == 2, BEHIND2, n))

    def total(m, carry):
        for k in range(2):

            @pl.when(jnp.logical_and(x == 1, 2 * m + k + ahead < n))
            def _(k=k):
                got_x(x + 1, 2 * m + k + ahead)

        def term(j, carry):
            @pl.when(jnp.logical_and(j > x, jnp.logical_or(x >= 2, j > x + 1)))
            def _():
                got_x(j, 2 * m)
                got_x(j, 2 * m + 1)

            hi, lo = split(xb[j, pl.ds(2 * m, 2)].reshape(2 * width, block))
            both = jnp.concatenate([hi, lo], axis=0)
            for t in range(3):
                at = slice(t * panel, (t + 1) * panel)
                first = dot(both, lh[4 + j, :, at])
                value = first[: 2 * width] + (first[2 * width :] + dot(hi, ll[4 + j, :, at]))
                sums[m, :, at] = jnp.where(j == 0, 0.0, sums[m, :, at]) + value
            return carry

        lax.fori_loop(0, 4, term, 0)
        send_sum(m).start()
        return carry

    def close_all():
        lax.fori_loop(0, 4, close_cross, 0)
        finish(7)

    def chunk(c, carry):
        early_x(c)

        def earlier(j, carry):
            @pl.when(j == x - 1)
            def _():
                got_x(j, c)
                update(c, j, 1)

            @pl.when(jnp.logical_and(j < x - 1, c % 2 == 0))
            def _():
                @pl.when(jnp.logical_not(early(j)))
                def _():
                    got_x(j, c)
                    got_x(j, c + 1)

                update(c, j, 2)

            return carry

        lax.fori_loop(0, x, earlier, 0)
        solve(c)

        @pl.when(jnp.logical_and(jnp.logical_and(is_a, x > 0), jnp.logical_and(c >= FAR, c - FAR < kept)))
        def _():
            far_on(4 + c - FAR)

        @pl.when(jnp.logical_and(is_a, c >= behind))
        def _():
            @pl.when(c == behind)
            def _():
                close_all()

            @pl.when((c - behind) % 2 == 1)
            def _():
                total((c - behind) // 2, 0)

        return carry

    lax.fori_loop(0, n, chunk, 0)
    for i in range(n, n + 3):

        @pl.when(is_b)
        def _():
            early_x(i)

    @pl.when(is_a)
    def _():
        @pl.when(x == 0)
        def _():
            def pass_second(c, carry):
                got_x(1, c)
                return carry

            def far_cross_group(s, carry):
                far_on(4 + s)
                return carry

            lax.fori_loop(0, kept, pass_on_cross, 0)
            lax.fori_loop(0, kept - 1, far_cross_group, 0)
            lax.fori_loop(0, n // 2, pass_second, 0)
            lax.fori_loop(kept - 1, kept, far_cross_group, 0)

        @pl.when(behind == n)
        def _():
            close_all()

        lax.fori_loop((n - behind) // 2, n // 2, total, 0)

    def sent_ring(slot, k=3):
        for a in range(2):
            for way in range(2):
                relay(slot, yh, z, send_z.at[slot, a, way], above, k).wait_send()
        far_up(slot, k).wait_send()
        far_down(slot, k).wait_send()

    def sent_own(slot, carry):
        def corner_sent():
            relay(slot, yh, z, send_y.at[slot, z], partner, 1).wait_send()
            sent_ring(slot, 1)
            to_twin(slot, 1).wait_send()

        def along_sent():
            for z_ in range(4):
                relay(slot, yh, z, send_y.at[slot, z_], partner).wait_send()
            for way in range(2):
                relay(slot, yh, z, send_z.at[slot, yh, way], above).wait_send()
            ring_one(slot, 0).wait_send()
            to_twin(slot).wait_send()

        def plain_sent():
            relay(slot, yh, z, send_y.at[slot, z], partner).wait_send()
            sent_ring(slot)
            to_twin(slot).wait_send()

        by_kind(slot, corner_sent, along_sent, plain_sent)
        return carry

    lax.fori_loop(0, x + 1, sent_own, 0)

    @pl.when(is_a)
    def _():
        def sent_used(s, carry):
            @pl.when(s < kept)
            def _():
                sent_ring(4 + s)

            to_twin(4 + s).wait_send()
            return carry

        lax.fori_loop(0, 4, sent_used, 0)

    @pl.when(is_b)
    def _():
        def sent_cross(s, carry):
            for far in range(2):
                over_y(panels(s), s, z, far).wait_send()

            @pl.when(s >= kept)
            def _():
                for way in range(2):
                    send_shard(panels(s), 4 + s, yh, z, send_z.at[4 + s, yh, way], above).wait_send()
                far_cross(s, 0).wait_send()
                for come in (up_z, down_z, (z + 2) % 4):
                    for far in range(2):
                        over_y(panels(s), s, come, far).wait_send()

            return carry

        lax.fori_loop(0, 4, sent_cross, 0)

    def sent_x(c, carry):
        @pl.when(own_east)
        def _():
            send_own_x(c, 0).wait_send()

        @pl.when(own_west(c))
        def _():
            send_own_x(c, 1).wait_send()

        @pl.when(far_east(c))
        def _():
            forward_x(x, c, 0).wait_send()

        @pl.when(far_west(c))
        def _():
            forward_x(x, c, 1).wait_send()

        @pl.when(jnp.logical_and(is_a, c % 2 == 0))
        def _():
            send_sum(c // 2).wait_send()

        return carry

    lax.fori_loop(0, n, sent_x, 0)


def body(factor, inverses, right_side):
    n = CHUNKS
    block, cols = right_side.shape
    panel = inverses.shape[1]
    part = factor.shape[2]
    width = cols // n
    turned = jnp.transpose(factor, (1, 2, 0))
    dma = pltpu.SemaphoreType.DMA
    vmem = pl.BlockSpec(memory_space=pltpu.VMEM)
    return pl.pallas_call(
        functools.partial(kernel, n),
        out_shape=jax.ShapeDtypeStruct((block, cols), F32),
        in_specs=[pl.BlockSpec(memory_space=pl.ANY), vmem, vmem],
        out_specs=vmem,
        scratch_shapes=[
            pltpu.VMEM((8, 2, 3, 8, part, block), F32),
            pltpu.VMEM((8, block, block), BF16),
            pltpu.VMEM((8, block, block), BF16),
            pltpu.VMEM((4, n, width, block), F32),
            pltpu.VMEM((n, width, block), F32),
            pltpu.VMEM((n // 2, 2 * width, block), F32),
            pltpu.VMEM((3, panel, panel), BF16),
            pltpu.VMEM((3, panel, panel), BF16),
            dma((6,)),
            dma((4, 4)),
            dma((4, 4, 2)),
            dma((8, 2, 2)),
            dma((8, 2)),
            dma((8,)),
            dma((8, 8)),
            dma((8,)),
            dma((n, 2)),
            dma((n, 2)),
            dma((4, n)),
            dma((n,)),
            dma((n,)),
        ],
        compiler_params=pltpu.CompilerParams(
            collective_id=0, has_side_effects=True, vmem_limit_bytes=60 * 1024 * 1024
        ),
    )(turned, inverses, right_side)


def solution(mesh):
    placed = (P("row", None, "rhs"), P("row", None, None), P("row", "rhs"))
    return jax.shard_map(
        body, mesh=mesh, in_specs=placed, out_specs=P("row", "rhs"), check_vma=False
    )
```
